256 devices in a mesh: bins: 64 (over z, y, core), slab: 4 (over x).
Axes of the slice: x: 4, y: 4, z: 8, core: 2. Of those that a mesh axis runs over, the one named last changes fastest.
Arguments:
- images: bfloat16 [1024, 128, 128], P('bins'), may hold values from -6 to 6
- projections: bfloat16 [512, 128, 128], P('bins'), may hold values from -6 to 6
- regions: int32 [1024, 2], P('bins'), may hold values from 0 to 63, all different within a row; in each aligned block of 16 rows (0 to 15, 16 to 31, ...) at most 2 rows name the same one
- offsets: int32 [2, 1024], P(None, 'bins'), may hold values from -12 to 12
- defocus: float32 [1024], P('bins'), may hold values from 0.5 to 3
- counts: int32 [512], P('bins'), may hold values from 0 to 399
- tilt_angle: float32 [512], P('bins'), may hold values from -3.140625 to 3.140625
Outputs:
- volume: float32 [128, 128, 128], P('bins', 'slab')
The draws below stay inside these ranges and needn't reach their ends.
Inputs may be any that keep to these rules, and one draw needn't show every extreme that they name: The 2 regions of a particle differ. At most 2 of the 16 particles of one index of bins name the same region, and on some index exactly 2 do.
All inputs are finite; a program needn't handle non-finite values.
Results may differ from the reference program's by a relative error of at most 0.0046.
Values may be sent and summed in bfloat16 or wider, within the bound.
A program may use at most 64 MiB of HBM per device.

```python
import math
import jax
import jax.numpy as jnp
import numpy as np
from jax import lax

BOX = 128
P_DEV = 16
BIN_DEV = 8
TOP = 2
CAP = 2
PARTICLES = 1024
NBINS_ALL = 512
N_BINS = 64


def draw_images(key, part):
    key = jax.random.fold_in(key, 11)
    return jnp.clip(jax.random.normal(key, (PARTICLES, BOX, BOX), jnp.float32), -6.0, 6.0).astype(jnp.bfloat16)


def draw_projections(key, part):
    key = jax.random.fold_in(key, 23)
    return jnp.clip(jax.random.normal(key, (NBINS_ALL, BOX, BOX), jnp.float32), -6.0, 6.0).astype(jnp.bfloat16)


def plant(array, stream_key, least, top_value):
    longest = array.shape.index(max(array.shape))
    spots = []
    for shift in (0, 1):
        where = [jax.random.randint(jax.random.fold_in(stream_key, axis), (), 0, length) for axis, length in enumerate(array.shape)]
        where[longest] = (where[longest] + shift) % array.shape[longest]
        spots.append(tuple(where))
    return array.at[spots[0]].set(least).at[spots[1]].set(top_value)


def block_scale(own_key, dims, cuts, low, high):
    factor_of = 1.0
    for axis_at, parts in cuts:
        steps = jax.random.uniform(jax.random.fold_in(jax.random.fold_in(own_key, 6), axis_at), (parts,), jnp.float32, low / len(cuts), high / len(cuts))
        factor_of = factor_of * jnp.repeat(jnp.exp(steps), dims[axis_at] // parts).reshape((-1,) + (1,) * (len(dims) - 1 - axis_at))
    return factor_of


def deal_out(own_key, own, number, rows, amount, top, reach, slope):
    ranking = jax.random.permutation(own_key, amount)
    heavy_load, ordinary = portions_of(amount, rows * top, reach, slope, True), portions_of(amount, rows * top, reach, slope, False)
    places = jnp.arange(amount)

    def named(tallies, turn):
        used = int((tallies > 0).sum())
        fixed = max(1, used // 4)
        passed = fixed + (places - fixed + turn * (used - fixed)) % max(1, amount - fixed)
        return jnp.zeros((amount,), jnp.int32).at[ranking[jnp.where(places < fixed, places, passed)]].set(jnp.asarray(tallies, jnp.int32))

    tallies = jnp.where(number % 4 == 0, named(heavy_load, number // 4), named(ordinary, number - number // 4 - 1))
    mixed = jax.random.permutation(jax.random.fold_in(own, 3), amount)
    giver, receiver = mixed[0:amount // 2 * 2:2], mixed[1:amount // 2 * 2:2]
    slack = jnp.minimum(tallies[giver] - 1, reach - tallies[receiver]) // 2
    slack = jnp.where((giver == ranking[0]) | (receiver == ranking[0]) | (tallies[receiver] == 0), 0, jnp.maximum(slack, 0))
    passed = jax.random.randint(jax.random.fold_in(own, 4), (amount // 2,), 0, 1 << 20) % (slack + 1)
    tallies = tallies.at[giver].add(-passed).at[receiver].add(passed)
    members = jnp.searchsorted(jnp.cumsum(tallies), jnp.arange(rows * top), side="right").astype(jnp.int32)
    table = members.reshape(top, rows).T
    table = table[jax.random.permutation(jax.random.fold_in(own, 1), rows)]
    turn = jax.random.randint(jax.random.fold_in(own, 2), (rows, 1), 0, top)
    return jnp.take_along_axis(table, (jnp.arange(top)[None, :] + turn) % top, axis=1)


def portions_of(number_of, total, most, slope, full):
    portions = [(1 << 20) // math.isqrt(standing ** slope) + 1 for standing in range(1, number_of + 1)]
    largest = most if full else min(most, max(-(-total // number_of), total * portions[0] // sum(portions)))
    least = 1 if total - largest >= number_of - 1 else 0
    given, spare = [largest] + [least] * (number_of - 1), total - largest - least * (number_of - 1)
    while spare > 0:
        candidates = [i for i in range(1, number_of) if given[i] < largest] or [i for i in range(1, number_of) if given[i] < most]
        pool, budget = sum([portions[i] for i in candidates]), spare
        for i in candidates:
            more = min(most - given[i], max(1, budget * portions[i] // pool), spare)
            given[i] = given[i] + more
            spare = spare - more
    return np.array(given)


def setup_inputs(seed: int = 0) -> dict:
    seeds = jax.random.split(jax.random.key(seed), 8)
    images = draw_images(jax.random.fold_in(seeds[7], 71), 0)
    projections = draw_projections(jax.random.fold_in(seeds[7], 71), 0)
    regions_keys = jax.random.split(jax.random.fold_in(seeds[2], 1), PARTICLES // P_DEV)
    regions_turns = jax.random.permutation(jax.random.fold_in(seeds[2], 3), PARTICLES // P_DEV)
    regions = jax.vmap(lambda own, number: deal_out(jax.random.fold_in(seeds[2], 2), own, number, P_DEV, N_BINS, TOP, CAP, 2))(regions_keys, regions_turns).reshape((PARTICLES, TOP))
    offsets = plant(jax.random.randint(seeds[3], (2, PARTICLES), -12, 13), jax.random.fold_in(seeds[3], 1), -12, 12).astype(jnp.int32)
    defocus = jnp.clip(jnp.exp(math.log(3.0) - 1.7917595 * jax.random.uniform(seeds[4], (PARTICLES,), jnp.float32) ** block_scale(seeds[4], (PARTICLES,), ((0, 64),), -0.2, 0.2)), 0.5, 3.0)
    counts = plant(jax.random.randint(seeds[5], (NBINS_ALL,), 0, 400), jax.random.fold_in(seeds[5], 1), 0, 399).astype(jnp.int32)
    tilt_angle = jnp.clip(jax.random.uniform(seeds[6], (NBINS_ALL,), jnp.float32, -3.140625, 3.140625), -3.140625, 3.140625)
    return dict(images=images, projections=projections, regions=regions, offsets=offsets, defocus=defocus, counts=counts, tilt_angle=tilt_angle)


AMP_COS = 0.1
AMP_SIN = 0.99498743710662
CHI_SCALE = 100.0
ENVELOPE = 8.0


def rounded(values):
    return lax.optimization_barrier(values.astype(jnp.bfloat16)).astype(jnp.float32)


def filter_block(stack, row_shift, col_shift, defocus):
    indices = jnp.arange(BOX, dtype=jnp.int32)

    def roll_one(single_image, shift_rows, shift_cols):
        moved = single_image[(indices - shift_rows) % BOX]
        return moved[:, (indices - shift_cols) % BOX]

    shifted = jax.vmap(roll_one)(stack, row_shift, col_shift).astype(jnp.float32)
    frequency = jnp.where(indices < BOX // 2, indices, indices - BOX).astype(jnp.float32) / BOX
    freq_squared = frequency[:, None] ** 2 + frequency[None, :] ** 2
    aberration = CHI_SCALE * defocus[:, None, None] * freq_squared[None]
    ctf_gain = -(AMP_SIN * jnp.sin(aberration) + AMP_COS * jnp.cos(aberration)) * jnp.exp(-ENVELOPE * freq_squared)[None]
    spectrum = jnp.fft.fft2(shifted)
    return jnp.real(jnp.fft.ifft2(spectrum * ctf_gain)).astype(jnp.bfloat16)


def reference(images, projections, regions, offsets, defocus, counts, tilt_angle):
    filtered = lax.map(lambda group_args: filter_block(*group_args),
                       (images.reshape(N_BINS, P_DEV, BOX, BOX), offsets[0].reshape(N_BINS, P_DEV),
                        offsets[1].reshape(N_BINS, P_DEV), defocus.reshape(N_BINS, P_DEV)))
    flat_images = lax.optimization_barrier(filtered.reshape(PARTICLES, BOX * BOX)).astype(jnp.float32)
    flat_proj = projections.reshape(NBINS_ALL, BOX * BOX).astype(jnp.float32)
    scores = jnp.dot(flat_images, flat_proj.T, precision=lax.Precision.HIGHEST)
    columns = (regions[:, :, None] * BIN_DEV + jnp.arange(BIN_DEV, dtype=jnp.int32)[None, None, :]).reshape(PARTICLES, TOP * BIN_DEV).astype(jnp.int32)
    log_prior = jnp.log(1.0 + counts.astype(jnp.float32))
    logits = jnp.take_along_axis(scores, columns, axis=1) / BOX + log_prior[columns]
    maximum = jnp.max(logits, axis=1, keepdims=True)
    log_norm = maximum + jnp.log(jnp.sum(jnp.exp(logits - maximum), axis=1, keepdims=True))
    posterior = rounded(jnp.exp(logits - log_norm))
    weight_table = jnp.zeros((NBINS_ALL, PARTICLES), jnp.float32).at[columns, jnp.arange(PARTICLES, dtype=jnp.int32)[:, None]].set(posterior)
    averages = rounded(jnp.dot(weight_table, flat_images, precision=lax.Precision.HIGHEST)).reshape(NBINS_ALL, BOX, BOX)
    centre = (BOX - 1) / 2.0
    axis_values = jnp.arange(BOX, dtype=jnp.int32).astype(jnp.float32)
    offsetted = axis_values - centre

    def add_bin(bin_index, running):
        landing = offsetted[None, :] * jnp.cos(tilt_angle[bin_index]) + offsetted[:, None] * jnp.sin(tilt_angle[bin_index]) + centre
        weights = rounded(jnp.maximum(0.0, 1.0 - jnp.abs(landing[None, :, :] - axis_values[:, None, None])))
        return running + jnp.dot(averages[bin_index], weights.reshape(BOX, BOX * BOX), precision=lax.Precision.HIGHEST)

    running = lax.fori_loop(0, NBINS_ALL, add_bin, jnp.zeros((BOX, BOX * BOX), jnp.float32))
    return running.reshape(BOX, BOX, BOX).transpose(1, 0, 2)
```

```python
import functools

import jax
import jax.numpy as jnp
import ml_dtypes
import numpy as np
from jax import lax
from jax.experimental import pallas as pl
from jax.experimental.pallas import tpu as pltpu
from jax.sharding import PartitionSpec as P

AMP_COS = 0.1
AMP_SIN = 0.99498743710662
CHI_SCALE = 100.0
ENVELOPE = 8.0
BOX = 128
PART = 16
BINS = 8
PLANE_GROUP = 8
MESH = pl.DeviceIdType.MESH
F32 = jnp.float32
BF16 = jnp.bfloat16


def tables(rows):
    i = np.arange(BOX)
    angle = 2.0 * np.pi / BOX * (i[:, None] * i[None, :] % BOX)
    cas = np.cos(angle) + np.sin(angle)
    high = cas.astype(ml_dtypes.bfloat16)
    low = (cas - high.astype(np.float64)).astype(ml_dtypes.bfloat16)
    right = np.concatenate([high, low], axis=1)
    left = np.concatenate([high, high, low], axis=1)
    last = np.concatenate([high, high, low], axis=0)
    wrapped = cas[np.arange(BOX + rows) % BOX].astype(np.float32)
    return right, left, last, wrapped


def split(value):
    high = value.astype(BF16)
    return high, (value - high.astype(F32)).astype(BF16)


def dot(a, b):
    return jnp.dot(a, b, preferred_element_type=F32)


def dot_nt(a, b):
    return lax.dot_general(a, b, (((1,), (1,)), ((), ())), preferred_element_type=F32)


def kernel(
    nz, nq, ns,
    offs, imgs, proj, meta, h_right, h_left, h_last, h_rows,
    out,
    gains, spec, staged, frames, refs, meta_p, meta_z, partial, stats, share, parts, total, aver, weights,
    give_e, give_o, take_e, take_o,
    s_mp, r_mp, s_pr, r_pr, s_mz, r_mz, s_rt, r_rt, s_lf, r_lf, s_x, r_x, s_st, r_st,
    s_rs, r_rs, s_ag, r_ag, s_e, r_e, s_o, r_o,
):
    rows = BOX // ns
    pairs = rows // 2
    half = rows // 2
    depth = 2 * nz * nq
    me = lax.axis_index("bins")
    slab = lax.axis_index("slab")
    z = me // nq
    q = lax.rem(me, nq)
    flip_q = nq - 1 - q
    centre = (BOX - 1) / 2.0

    def at_q(k):
        other = lax.rem(q + k, nq)
        return other, (z * nq + other, slab)

    def at_z(k):
        other = lax.rem(z + k, nz)
        return other, (other * nq + q, slab)

    barrier = pltpu.get_barrier_semaphore()
    partners = [at_q(k)[1] for k in range(1, nq)] + [at_z(k)[1] for k in range(1, nz)]
    partners += [(lax.rem(z + k, nz) * nq + flip_q, slab) for k in range(1, nz)]
    partners += [(me, lax.rem(slab + k, ns)) for k in range(1, ns)]
    for device in partners:
        pl.semaphore_signal(barrier, inc=1, device_id=device, device_id_type=MESH)

    lane = lax.broadcasted_iota(jnp.int32, (8, BOX), 1)
    meta_p[q, 0:8, :] = jnp.log(1.0 + meta[24:32, :])
    meta_p[q, 8:16, :] = jnp.cos(meta[16:24, :])
    meta_p[q, 16:24, :] = jnp.sin(meta[16:24, :])
    meta_z[z] = jnp.where(lane // PART == z, meta[32:40, :], 0.0)

    first_row = pl.multiple_of(slab * rows, rows)
    for g in range(BINS):
        staged[g * rows:(g + 1) * rows, :] = proj[g, pl.ds(first_row, rows), :].astype(F32)
    for r in range(pairs):
        even = staged[pl.ds(2 * r, BINS, stride=rows), :]
        odd = staged[pl.ds(2 * r + 1, BINS, stride=rows), :]
        refs[q, r] = jnp.concatenate([even, odd], axis=0).astype(BF16)

    index = lax.broadcasted_iota(jnp.int32, (PART, BOX), 1)
    freq = jnp.where(index < BOX // 2, index, index - BOX).astype(F32) / BOX
    square = freq * freq
    phase = CHI_SCALE * meta[0:PART, :] * square
    fade = jnp.exp(-ENVELOPE * square)
    sine, cosine = jnp.sin(phase), jnp.cos(phase)
    scale = -1.0 / (BOX * BOX)
    gains[0] = scale * fade * (AMP_SIN * sine + AMP_COS * cosine)
    gains[1] = scale * fade * (AMP_SIN * cosine - AMP_COS * sine)
    gains[2] = fade * cosine
    gains[3] = fade * sine

    def filter_one(p):
        t = dot(imgs[p], h_right[...])
        th, tl = split(t[:, :BOX] + t[:, BOX:])
        s = dot(h_left[...], jnp.concatenate([th, tl, th], axis=0))
        start = lax.rem(slab * rows - offs[0, p] + 2 * BOX, BOX)
        a = h_rows[pl.ds(start, rows), :]
        lh, ll = split(jnp.concatenate([a * gains[0, pl.ds(p, 1), :], a * gains[1, pl.ds(p, 1), :]], axis=1))
        rh, rl = split(jnp.concatenate([s * gains[2, pl.ds(p, 1), :], s * gains[3, pl.ds(p, 1), :]], axis=0))
        spec[pl.ds(pl.multiple_of(p * rows, rows), rows), :] = dot(lh, rh) + dot(lh, rl) + dot(ll, rh)

    def filter_some(step, carry):
        for k in range(4):
            filter_one(step * 4 + k)
        return carry

    lax.fori_loop(0, PART // 4, filter_some, 0)
    qh, ql = split(spec[...])
    plain = dot(jnp.concatenate([qh, ql, qh], axis=1), h_last[...])
    for p in range(PART):
        shift = lax.rem(offs[1, p] + BOX, BOX)
        staged[p * rows:(p + 1) * rows, :] = pltpu.roll(plain[p * rows:(p + 1) * rows, :], shift, 1)
    for r in range(rows):
        frames[z, r] = staged[pl.ds(r, PART, stride=rows), :].astype(BF16)

    pl.semaphore_wait(barrier, len(partners))

    def to_q(buf, send, recv, k):
        device = at_q(k)[1]
        return pltpu.make_async_remote_copy(buf.at[q], buf.at[q], send.at[k], recv.at[k], device_id=device, device_id_type=MESH)

    def to_z(buf, send, recv, k):
        device = at_z(k)[1]
        return pltpu.make_async_remote_copy(buf.at[z], buf.at[z], send.at[k], recv.at[k], device_id=device, device_id_type=MESH)

    def ring(step, sign, send, recv):
        source = lax.rem(z + (nz - sign * (step // 2)), nz)
        piece = step % 2 if sign > 0 else 1 - step % 2
        ref = frames.at[source, pl.ds(piece * half, half)]
        device = (lax.rem(z + nz + sign, nz) * nq + q, slab)
        return pltpu.make_async_remote_copy(ref, ref, send.at[step], recv.at[step], device_id=device, device_id_type=MESH)

    def right(step):
        return ring(step, 1, s_rt, r_rt)

    def left(step):
        return ring(step, -1, s_lf, r_lf)

    steps = nz - 1
    for step in range(min(2, steps)):
        right(step).start()
        left(step).start()
    for k in range(1, nq):
        to_q(meta_p, s_mp, r_mp, k).start()
    for k in range(1, nz):
        to_z(meta_z, s_mz, r_mz, k).start()
    for k in range(1, nq):
        to_q(refs, s_pr, r_pr, k).start()
    for k in range(1, nq):
        to_q(meta_p, s_mp, r_mp, k).wait()

    column = lax.broadcasted_iota(jnp.int32, (1, BOX), 1).astype(F32) - centre
    height = lax.broadcasted_iota(jnp.int32, (BOX, BOX), 0).astype(F32)

    def weigh(j):
        def one(g, carry):
            cosr = meta_p[j, pl.ds(8 + g, 1), :]
            sinr = meta_p[j, pl.ds(16 + g, 1), :]
            base = pl.multiple_of((j * BINS + g) * BOX, BOX)
            for k in range(nz):
                plane = 2 * (lax.rem(z + k, nz) * nq + q)
                away = plane.astype(F32) - (depth - 1) / 2.0
                landing = column * cosr + away * sinr + centre
                w = jnp.maximum(0.0, 1.0 - jnp.abs(landing - height))
                weights[pl.ds(base, BOX), k * BOX:(k + 1) * BOX] = w.astype(BF16)
            return carry

        lax.fori_loop(0, BINS, one, 0)

    for step in range(steps):
        right(step).wait_recv()
        if step + 2 < steps:
            right(step + 2).start()
        left(step).wait_recv()
        if step + 2 < steps:
            left(step + 2).start()
        if step < nq:
            weigh(step)
    for j in range(steps, nq):
        weigh(j)

    for k in range(1, nq):
        to_q(refs, s_pr, r_pr, k).wait()
    for k in range(1, nz):
        to_z(meta_z, s_mz, r_mz, k).wait()
    for step in range(steps):
        right(step).wait_send()
        left(step).wait_send()

    lanes = nz * PART

    def frame(r):
        return frames[:, r].reshape(lanes, BOX)

    def score(r, carry):
        even, odd = carry
        a = refs[:, r].reshape(nq * 2 * BINS, BOX)
        return even + dot_nt(a, frame(2 * r)), odd + dot_nt(a, frame(2 * r + 1))

    zero = jnp.zeros((nq * 2 * BINS, lanes), F32)
    even, odd = lax.fori_loop(0, pairs, score, (zero, zero), unroll=4)
    even = even.reshape(nq, 2, BINS, lanes)[:, 0]
    odd = odd.reshape(nq, 2, BINS, lanes)[:, 1]
    partial[slab] = (even + odd).reshape(nq * BINS, lanes)

    def to_x(k):
        device = (me, lax.rem(slab + k, ns))
        return pltpu.make_async_remote_copy(
            partial.at[slab], partial.at[slab], s_x.at[k], r_x.at[k], device_id=device, device_id_type=MESH
        )

    for k in range(1, ns):
        to_x(k).start()
    for k in range(1, ns):
        to_x(k).wait()
    scores = partial[0]
    for k in range(1, ns):
        scores = scores + partial[k]
    prior = meta_p[:, 0:8, :][:, :, :lanes].reshape(nq * BINS, lanes)
    logits = scores / BOX + prior
    named = meta_z[0]
    for k in range(1, nz):
        named = named + meta_z[k]
    owner = (lax.broadcasted_iota(jnp.int32, (nq * BINS, lanes), 0) // BINS + z * nq).astype(F32)
    wanted = (owner == named[0:1, :lanes]) | (owner == named[1:2, :lanes])
    low = jnp.float32(-3.0e38)
    top = jnp.max(jnp.where(wanted, logits, low), axis=0, keepdims=True)
    summed = jnp.sum(jnp.where(wanted, jnp.exp(jnp.where(wanted, logits - top, 0.0)), 0.0), axis=0, keepdims=True)
    stats[z, 0:1, :lanes] = top
    stats[z, 1:2, :lanes] = summed
    for k in range(1, nz):
        to_z(stats, s_st, r_st, k).start()
    for k in range(1, nz):
        to_z(stats, s_st, r_st, k).wait()
    tops = stats[:, 0, :lanes]
    sums = stats[:, 1, :lanes]
    best = jnp.max(tops, axis=0, keepdims=True)
    norm = best + jnp.log(jnp.sum(sums * jnp.exp(tops - best), axis=0, keepdims=True))
    posterior = jnp.where(wanted, jnp.exp(jnp.where(wanted, logits - norm, 0.0)), 0.0).astype(BF16)

    def average(r, carry):
        a = dot(posterior, frame(2 * r)).reshape(nq, BINS, BOX)
        b = dot(posterior, frame(2 * r + 1)).reshape(nq, BINS, BOX)
        share[:, r] = jnp.concatenate([a, b], axis=1).astype(BF16)
        return carry

    lax.fori_loop(0, pairs, average, 0, unroll=4)

    def to_owner(k):
        other, device = at_q(k)
        return pltpu.make_async_remote_copy(
            share.at[other], parts.at[k], s_rs.at[k], r_rs.at[k], device_id=device, device_id_type=MESH
        )

    for k in range(1, nq):
        to_owner(k).start()
    for k in range(1, nq):
        to_owner(k).wait()

    def add_up(r, carry):
        value = share[q, r].astype(F32)
        for k in range(1, nq):
            value = value + parts[k, r].astype(F32)
        total[pl.ds(pl.multiple_of(r * 2 * BINS, 2 * BINS), 2 * BINS), :] = value
        return carry

    lax.fori_loop(0, pairs, add_up, 0, unroll=4)
    mine = pl.multiple_of(q * BINS * BOX, BINS * BOX)
    for g in range(BINS):
        block = total[pl.ds(g, rows, stride=BINS), :].astype(BF16)
        aver[0:rows, pl.ds(pl.multiple_of(mine + g * BOX, BOX), BOX)] = block

    def to_group(k):
        ref = aver.at[pl.ds(0, rows), pl.ds(mine, BINS * BOX)]
        device = at_q(k)[1]
        return pltpu.make_async_remote_copy(ref, ref, s_ag.at[k], r_ag.at[k], device_id=device, device_id_type=MESH)

    for k in range(1, nq):
        to_group(k).start()

    mirror = (
        lax.broadcasted_iota(jnp.int32, (BOX, BOX), 0) + lax.broadcasted_iota(jnp.int32, (BOX, BOX), 1) == BOX - 1
    ).astype(F32).astype(BF16)

    def reverse(k):
        base = pl.multiple_of(lax.rem(q - k + nq, nq) * BINS * BOX, BINS * BOX)
        for g in range(BINS):
            at = pl.ds(pl.multiple_of(base + g * BOX, BOX), BOX)
            aver[rows:2 * rows, at] = dot(aver[0:rows, at], mirror).astype(BF16)

    reverse(0)
    for k in range(1, nq):
        to_group(k).wait()
        reverse(k)

    def even_copy(k):
        return pltpu.make_async_remote_copy(
            give_e.at[k], take_e.at[k], s_e.at[k], r_e.at[k], device_id=at_z(k)[1], device_id_type=MESH
        )

    def odd_copy(k):
        device = ((nz - 1 - lax.rem(z + k, nz)) * nq + flip_q, slab)
        return pltpu.make_async_remote_copy(
            give_o.at[k], take_o.at[k], s_o.at[k], r_o.at[k], device_id=device, device_id_type=MESH
        )

    order = sorted(range(nz // 2), key=lambda pair: -min(2 * pair, nz - 2 * pair))
    for pair in order:
        block = dot(aver[...], weights[:, 2 * pair * BOX:(2 * pair + 2) * BOX])
        for k in (2 * pair, 2 * pair + 1):
            at = (k - 2 * pair) * BOX
            give_e[k] = block[:rows, at:at + BOX].astype(BF16)
            give_o[k] = block[rows:, at:at + BOX].astype(BF16)
            odd_copy(k).start()
            if k:
                even_copy(k).start()

    for k in range(nz):
        odd_copy(k).wait()
        if k:
            even_copy(k).wait()
    value = give_e[0].astype(F32)
    for k in range(1, nz):
        value = value + take_e[k].astype(F32)
    out[0] = value
    value = take_o[0].astype(F32)
    for k in range(1, nz):
        value = value + take_o[k].astype(F32)
    high, rest = split(value)
    middle = (value - high.astype(F32)).astype(BF16)
    lowest = (value - high.astype(F32) - middle.astype(F32)).astype(BF16)
    out[1] = dot(jnp.concatenate([high, middle, lowest], axis=1), jnp.concatenate([mirror] * 3, axis=0))


def body(nz, nq, ns, images, projections, regions, offsets, defocus, counts, tilt_angle):
    rows = BOX // ns
    pairs = rows // 2
    wide = lambda vector: jnp.broadcast_to(vector.astype(F32)[:, None], (vector.shape[0], BOX))
    named = jnp.tile(regions.astype(F32).T, (1, BOX // PART))
    meta = jnp.concatenate(
        [wide(defocus), wide(tilt_angle), wide(counts), jnp.pad(named, ((0, 6), (0, 0)))], axis=0
    )
    vmem = pl.BlockSpec(memory_space=pltpu.VMEM)
    dma = pltpu.SemaphoreType.DMA
    scratch = [
        pltpu.VMEM((4, PART, BOX), F32),
        pltpu.VMEM((PART * rows, BOX), F32),
        pltpu.VMEM((PART * rows, BOX), F32),
        pltpu.VMEM((nz, rows, PART, BOX), BF16),
        pltpu.VMEM((nq, pairs, 2 * BINS, BOX), BF16),
        pltpu.VMEM((nq, 24, BOX), F32),
        pltpu.VMEM((nz, 8, BOX), F32),
        pltpu.VMEM((ns, nq * BINS, nz * PART), F32),
        pltpu.VMEM((nz, 8, BOX), F32),
        pltpu.VMEM((nq, pairs, 2 * BINS, BOX), BF16),
        pltpu.VMEM((nq, pairs, 2 * BINS, BOX), BF16),
        pltpu.VMEM((rows * BINS, BOX), F32),
        pltpu.VMEM((2 * rows, nq * BINS * BOX), BF16),
        pltpu.VMEM((nq * BINS * BOX, nz * BOX), BF16),
        pltpu.VMEM((nz, rows, BOX), BF16),
        pltpu.VMEM((nz, rows, BOX), BF16),
        pltpu.VMEM((nz, rows, BOX), BF16),
        pltpu.VMEM((nz, rows, BOX), BF16),
    ]
    for count in (nq, nq, nz, nz, nz, ns, nz, nq, nq, nz, nz):
        scratch += [dma((count,)), dma((count,))]
    return pl.pallas_call(
        functools.partial(kernel, nz, nq, ns),
        out_shape=jax.ShapeDtypeStruct((2, rows, BOX), F32),
        in_specs=[pl.BlockSpec(memory_space=pltpu.SMEM)] + [vmem] * 7,
        out_specs=vmem,
        scratch_shapes=scratch,
        compiler_params=pltpu.CompilerParams(
            collective_id=0, has_side_effects=True, vmem_limit_bytes=48 * 1024 * 1024
        ),
    )(offsets, images, projections, meta, *(jnp.asarray(table) for table in tables(rows)))


def solution(mesh):
    nq = PLANE_GROUP
    nz = mesh.shape["bins"] // nq
    ns = mesh.shape["slab"]
    in_specs = (
        P("bins", None, None),
        P("bins", None, None),
        P("bins", None),
        P(None, "bins"),
        P("bins"),
        P("bins"),
        P("bins"),
    )
    return jax.shard_map(
        functools.partial(body, nz, nq, ns),
        mesh=mesh,
        in_specs=in_specs,
        out_specs=P("bins", "slab", None),
        check_vma=False,
    )
```

```python
import functools

import jax
import jax.numpy as jnp
import ml_dtypes
import numpy as np
from jax import lax
from jax.experimental import pallas as pl
from jax.experimental.pallas import tpu as pltpu
from jax.sharding import PartitionSpec as P

AMP_COS = 0.1
AMP_SIN = 0.99498743710662
CHI_SCALE = 100.0
ENVELOPE = 8.0
BOX = 128
PART = 16
BINS = 8
PLANE_GROUP = 8
PIECES = 4
MESH = pl.DeviceIdType.MESH
F32 = jnp.float32
BF16 = jnp.bfloat16


def tables(rows):
    i = np.arange(BOX)
    angle = 2.0 * np.pi / BOX * (i[:, None] * i[None, :] % BOX)
    cas = np.cos(angle) + np.sin(angle)
    high = cas.astype(ml_dtypes.bfloat16)
    low = (cas - high.astype(np.float64)).astype(ml_dtypes.bfloat16)
    right = np.concatenate([high, low], axis=1)
    left = np.concatenate([high, high, low], axis=1)
    last = np.concatenate([high, high, low], axis=0)
    wrapped = cas[np.arange(BOX + rows) % BOX].astype(np.float32)
    return right, left, last, wrapped


def split(value):
    high = value.astype(BF16)
    return high, (value - high.astype(F32)).astype(BF16)


def dot(a, b):
    return jnp.dot(a, b, preferred_element_type=F32)


def dot_nt(a, b):
    return lax.dot_general(a, b, (((1,), (1,)), ((), ())), preferred_element_type=F32)


def kernel(
    nz, nq, ns,
    regions, offs, defocus, counts, tilt, images_hbm, proj_hbm, right_hbm, left_hbm, last_hbm, rows_hbm,
    out,
    imgs, proj, h_right, h_left, h_last, h_rows,
    gains, spec, staged, frames, refs, meta_p, meta_z, partial, stats, share, from_core, send_y, from_y, total,
    aver, weights, planes, give_e, give_o, take_e, take_o,
    s_in, s_mp, r_mp, s_pr, r_pr, s_mz, r_mz, s_rt, r_rt, s_lf, r_lf, s_x, r_x, s_st, r_st,
    s_rc, r_rc, s_ry, r_ry, s_ac, r_ac, s_ay, r_ay, s_e, r_e, s_o, r_o,
):
    rows = BOX // ns
    pairs = rows // 2
    ny = nq // 2
    quarter = rows // PIECES
    depth = 2 * nz * nq
    me = lax.axis_index("bins")
    slab = lax.axis_index("slab")
    z = me // nq
    q = lax.rem(me, nq)
    flip_q = nq - 1 - q
    y = q // 2
    core = lax.rem(q, 2)
    other_core = (z * nq + 2 * y + 1 - core, slab)
    centre = (BOX - 1) / 2.0

    def at_q(k):
        other = lax.rem(q + k, nq)
        return other, (z * nq + other, slab)

    def at_z(k):
        other = lax.rem(z + k, nz)
        return other, (other * nq + q, slab)

    def at_y(k):
        other = lax.rem(y + k, ny)
        return other, (z * nq + 2 * other + core, slab)

    first_row = pl.multiple_of(slab * rows, rows)
    loads = [
        pltpu.make_async_copy(src, dst, s_in.at[i])
        for i, (src, dst) in enumerate(
            (
                (images_hbm, imgs),
                (right_hbm, h_right),
                (left_hbm, h_left),
                (rows_hbm, h_rows),
                (last_hbm, h_last),
                (proj_hbm.at[:, pl.ds(first_row, rows)], proj),
            )
        )
    ]
    for load in loads:
        load.start()

    barrier = pltpu.get_barrier_semaphore()
    partners = [at_q(k)[1] for k in range(1, nq)] + [at_z(k)[1] for k in range(1, nz)]
    partners += [(lax.rem(z + k, nz) * nq + flip_q, slab) for k in range(1, nz)]
    partners += [(me, lax.rem(slab + k, ns)) for k in range(1, ns)]
    for device in partners:
        pl.semaphore_signal(barrier, inc=1, device_id=device, device_id_type=MESH)

    lane = lax.broadcasted_iota(jnp.int32, (8, BOX), 1)
    line = lax.broadcasted_iota(jnp.int32, (8, BOX), 0)
    angle = jnp.zeros((8, BOX), F32)
    count = jnp.zeros((8, BOX), jnp.int32)
    for g in range(BINS):
        angle = jnp.where(line == g, tilt[g], angle)
        count = jnp.where(line == g, counts[g], count)
    meta_p[q, 0:8, :] = jnp.log(1.0 + count.astype(F32))
    meta_p[q, 8:16, :] = jnp.cos(angle)
    meta_p[q, 16:24, :] = jnp.sin(angle)
    named = jnp.zeros((8, BOX), jnp.int32)
    for p in range(PART):
        for t in range(2):
            named = jnp.where((lane == z * PART + p) & (line == t), regions[p, t], named)
    meta_z[z] = named

    index = lax.broadcasted_iota(jnp.int32, (PART, BOX), 1)
    which = lax.broadcasted_iota(jnp.int32, (PART, BOX), 0)
    blur = jnp.zeros((PART, BOX), F32)
    for p in range(PART):
        blur = jnp.where(which == p, defocus[p], blur)
    freq = jnp.where(index < BOX // 2, index, index - BOX).astype(F32) / BOX
    square = freq * freq
    phase = CHI_SCALE * blur * square
    fade = jnp.exp(-ENVELOPE * square)
    sine, cosine = jnp.sin(phase), jnp.cos(phase)
    scale = -1.0 / (BOX * BOX)
    gains[0] = scale * fade * (AMP_SIN * sine + AMP_COS * cosine)
    gains[1] = scale * fade * (AMP_SIN * cosine - AMP_COS * sine)
    gains[2] = fade * cosine
    gains[3] = fade * sine

    loads[5].wait()
    for g in range(BINS):
        staged[g * rows:(g + 1) * rows, :] = proj[g].astype(F32)
    for r in range(pairs):
        even = staged[pl.ds(2 * r, BINS, stride=rows), :]
        odd = staged[pl.ds(2 * r + 1, BINS, stride=rows), :]
        refs[q, r] = jnp.concatenate([even, odd], axis=0).astype(BF16)

    def filter_one(p):
        t = dot(imgs[p], h_right[...])
        th, tl = split(t[:, :BOX] + t[:, BOX:])
        s = dot(h_left[...], jnp.concatenate([th, tl, th], axis=0))
        start = lax.rem(slab * rows - offs[0, p] + 2 * BOX, BOX)
        a = h_rows[pl.ds(start, rows), :]
        lh, ll = split(jnp.concatenate([a * gains[0, pl.ds(p, 1), :], a * gains[1, pl.ds(p, 1), :]], axis=1))
        rh, rl = split(jnp.concatenate([s * gains[2, pl.ds(p, 1), :], s * gains[3, pl.ds(p, 1), :]], axis=0))
        spec[pl.ds(pl.multiple_of(p * rows, rows), rows), :] = dot(lh, rh) + dot(lh, rl) + dot(ll, rh)

    def filter_some(step, carry):
        for k in range(4):
            filter_one(step * 4 + k)
        return carry

    for load in loads[:4]:
        load.wait()
    lax.fori_loop(0, PART // 4, filter_some, 0)
    loads[4].wait()
    qh, ql = split(spec[...])
    plain = dot(jnp.concatenate([qh, ql, qh], axis=1), h_last[...])
    for p in range(PART):
        shift = lax.rem(offs[1, p] + BOX, BOX)
        staged[p * rows:(p + 1) * rows, :] = pltpu.roll(plain[p * rows:(p + 1) * rows, :], shift, 1)
    for r in range(rows):
        frames[z, r] = staged[pl.ds(r, PART, stride=rows), :].astype(BF16)

    pl.semaphore_wait(barrier, len(partners))

    def to_q(buf, send, recv, k):
        device = at_q(k)[1]
        return pltpu.make_async_remote_copy(buf.at[q], buf.at[q], send.at[k], recv.at[k], device_id=device, device_id_type=MESH)

    def to_z(buf, send, recv, k):
        device = at_z(k)[1]
        return pltpu.make_async_remote_copy(buf.at[z], buf.at[z], send.at[k], recv.at[k], device_id=device, device_id_type=MESH)

    def ring(step, sign, send, recv):
        source = lax.rem(z + (nz - sign * (step // PIECES)), nz)
        piece = step % PIECES if sign > 0 else PIECES - 1 - step % PIECES
        ref = frames.at[source, pl.ds(piece * quarter, quarter)]
        device = (lax.rem(z + nz + sign, nz) * nq + q, slab)
        return pltpu.make_async_remote_copy(ref, ref, send.at[step], recv.at[step], device_id=device, device_id_type=MESH)

    def right(step):
        return ring(step, 1, s_rt, r_rt)

    def left(step):
        return ring(step, -1, s_lf, r_lf)

    steps = PIECES * (nz - 1) // 2
    for step in range(PIECES):
        right(step).start()
        left(step).start()
    for k in range(1, nq):
        to_q(meta_p, s_mp, r_mp, k).start()
    for k in range(1, nz):
        to_z(meta_z, s_mz, r_mz, k).start()
    for k in range(1, nq):
        to_q(refs, s_pr, r_pr, k).start()
    for k in range(1, nq):
        to_q(meta_p, s_mp, r_mp, k).wait()

    column = lax.broadcasted_iota(jnp.int32, (1, BOX), 1).astype(F32) - centre
    height = lax.broadcasted_iota(jnp.int32, (BOX, BOX), 0).astype(F32)

    def weigh(unit):
        j = unit // 2

        def one(g, carry):
            cosr = meta_p[j, pl.ds(8 + g, 1), :]
            sinr = meta_p[j, pl.ds(16 + g, 1), :]
            base = pl.multiple_of((j * BINS + g) * BOX, BOX)
            for k in range(nz):
                plane = 2 * (lax.rem(z + k, nz) * nq + q)
                away = plane.astype(F32) - (depth - 1) / 2.0
                landing = column * cosr + away * sinr + centre
                w = jnp.maximum(0.0, 1.0 - jnp.abs(landing - height))
                weights[pl.ds(base, BOX), k * BOX:(k + 1) * BOX] = w.astype(BF16)
            return carry

        first = unit % 2 * (BINS // 2)
        lax.fori_loop(first, first + BINS // 2, one, 0)

    units = 2 * nq
    for step in range(steps):
        right(step).wait_recv()
        if step + PIECES < steps:
            right(step + PIECES).start()
        left(step).wait_recv()
        if step + PIECES < steps:
            left(step + PIECES).start()
        for unit in range(step * units // steps, (step + 1) * units // steps):
            weigh(unit)

    for k in range(1, nq):
        to_q(refs, s_pr, r_pr, k).wait()
    for k in range(1, nz):
        to_z(meta_z, s_mz, r_mz, k).wait()
    for step in range(steps):
        right(step).wait_send()
        left(step).wait_send()

    lanes = nz * PART

    def frame(r):
        return frames[:, r].reshape(lanes, BOX)

    def score(r, carry):
        even, odd = carry
        a = refs[:, r].reshape(nq * 2 * BINS, BOX)
        return even + dot_nt(a, frame(2 * r)), odd + dot_nt(a, frame(2 * r + 1))

    zero = jnp.zeros((nq * 2 * BINS, lanes), F32)
    even, odd = lax.fori_loop(0, pairs, score, (zero, zero), unroll=4)
    even = even.reshape(nq, 2, BINS, lanes)[:, 0]
    odd = odd.reshape(nq, 2, BINS, lanes)[:, 1]
    scores = even + odd

    named = meta_z[0]
    for k in range(1, nz):
        named = named + meta_z[k]
    prior = meta_p[:, 0:8, :lanes]
    held, priors = [], []
    for t in range(2):
        place = named[t:t + 1, :lanes] - z * nq
        chosen = jnp.zeros((BINS, lanes), F32)
        chance = jnp.zeros((BINS, lanes), F32)
        for j in range(nq):
            chosen = jnp.where(place == j, scores[j], chosen)
            chance = jnp.where(place == j, prior[j], chance)
        partial[slab, t * BINS:(t + 1) * BINS, :] = chosen
        priors.append(chance)
        held.append((place >= 0) & (place < nq))

    def to_x(k):
        device = (me, lax.rem(slab + k, ns))
        return pltpu.make_async_remote_copy(
            partial.at[slab], partial.at[slab], s_x.at[k], r_x.at[k], device_id=device, device_id_type=MESH
        )

    for k in range(1, ns):
        to_x(k).start()
    for k in range(1, ns):
        to_x(k).wait()
    scores = partial[0]
    for k in range(1, ns):
        scores = scores + partial[k]
    low = jnp.float32(-3.0e38)
    logits = [scores[t * BINS:(t + 1) * BINS] / BOX + priors[t] for t in range(2)]
    tops = [jnp.where(held[t], jnp.max(logits[t], axis=0, keepdims=True), low) for t in range(2)]
    top = jnp.maximum(tops[0], tops[1])
    summed = jnp.zeros((1, lanes), F32)
    for t in range(2):
        grown = jnp.exp(jnp.where(held[t], logits[t] - top, low))
        summed = summed + jnp.sum(grown, axis=0, keepdims=True)
    stats[z, 0:1, :lanes] = top
    stats[z, 1:2, :lanes] = summed
    for k in range(1, nz):
        to_z(stats, s_st, r_st, k).start()
    for k in range(1, nz):
        to_z(stats, s_st, r_st, k).wait()
    best = stats[0, 0:1, :lanes]
    for k in range(1, nz):
        best = jnp.maximum(best, stats[k, 0:1, :lanes])
    whole = jnp.zeros((1, lanes), F32)
    for k in range(nz):
        whole = whole + stats[k, 1:2, :lanes] * jnp.exp(stats[k, 0:1, :lanes] - best)
    norm = best + jnp.log(whole)
    chances = [jnp.exp(jnp.where(held[t], logits[t] - norm, low)) for t in range(2)]
    posterior = []
    for j in range(nq):
        value = jnp.zeros((BINS, lanes), F32)
        for t in range(2):
            place = named[t:t + 1, :lanes] - z * nq
            value = jnp.where(place == j, chances[t], value)
        posterior.append(value)
    posterior = jnp.concatenate(posterior, axis=0).astype(BF16)

    def average(r, carry):
        a = dot(posterior, frame(r)).reshape(ny, 2, BINS, BOX)
        share[0, :, r] = a[:, 0]
        share[1, :, r] = a[:, 1]
        return carry

    lax.fori_loop(0, rows, average, 0, unroll=8)

    def to_core(k):
        place = at_y(k)[0]
        return pltpu.make_async_remote_copy(
            share.at[1 - core, place], from_core.at[place], s_rc.at[k], r_rc.at[k],
            device_id=other_core, device_id_type=MESH,
        )

    def to_owner(k):
        return pltpu.make_async_remote_copy(
            send_y.at[k], from_y.at[k], s_ry.at[k], r_ry.at[k], device_id=at_y(k)[1], device_id_type=MESH
        )

    far_first = sorted(range(1, ny), key=lambda k: -min(k, ny - k))
    for k in far_first + [0]:
        to_core(k).start()
    for k in far_first:
        place = at_y(k)[0]
        to_core(k).wait_recv()

        def pack(r, carry):
            a = share[core, place, 2 * r] + from_core[place, 2 * r]
            b = share[core, place, 2 * r + 1] + from_core[place, 2 * r + 1]
            send_y[k, r] = jnp.concatenate([a, b], axis=0).astype(BF16)
            return carry

        lax.fori_loop(0, pairs, pack, 0, unroll=8)
        to_owner(k).start()
    to_core(0).wait_recv()
    for k in range(1, ny):
        to_owner(k).wait_recv()

    def add_up(r, carry):
        a = share[core, y, 2 * r] + from_core[y, 2 * r]
        b = share[core, y, 2 * r + 1] + from_core[y, 2 * r + 1]
        value = jnp.concatenate([a, b], axis=0)
        for k in range(1, ny):
            value = value + from_y[k, r].astype(F32)
        total[pl.ds(pl.multiple_of(r * 2 * BINS, 2 * BINS), 2 * BINS), :] = value
        return carry

    lax.fori_loop(0, pairs, add_up, 0, unroll=8)
    span = BINS * BOX
    mine = pl.multiple_of(q * span, span)
    for g in range(BINS):
        block = total[pl.ds(g, rows, stride=BINS), :].astype(BF16)
        aver[0:rows, pl.ds(pl.multiple_of(mine + g * BOX, BOX), BOX)] = block

    def block_of(place, which):
        return pl.multiple_of((2 * place + which) * span, span)

    def along_y(k):
        ref = aver.at[pl.ds(0, rows), pl.ds(mine, span)]
        return pltpu.make_async_remote_copy(ref, ref, s_ay.at[k], r_ay.at[k], device_id=at_y(k)[1], device_id_type=MESH)

    def across(k):
        ref = aver.at[pl.ds(0, rows), pl.ds(block_of(lax.rem(y - k + ny, ny), core), span)]
        return pltpu.make_async_remote_copy(ref, ref, s_ac.at[k], r_ac.at[k], device_id=other_core, device_id_type=MESH)

    for k in far_first:
        along_y(k).start()
    across(0).start()

    mirror = (
        lax.broadcasted_iota(jnp.int32, (BOX, BOX), 0) + lax.broadcasted_iota(jnp.int32, (BOX, BOX), 1) == BOX - 1
    ).astype(F32).astype(BF16)

    def reverse(base):
        tiles = [aver[0:rows, pl.ds(pl.multiple_of(base + g * BOX, BOX), BOX)] for g in range(BINS)]
        turned = dot(jnp.concatenate(tiles, axis=0), mirror).astype(BF16)
        for g in range(BINS):
            aver[rows:2 * rows, pl.ds(pl.multiple_of(base + g * BOX, BOX), BOX)] = turned[g * rows:(g + 1) * rows]

    def project(base, lanes_at):
        return dot(aver[:, pl.ds(base, span)], weights[pl.ds(base, span), lanes_at])

    def add_block(base, first):
        reverse(base)
        for pair in range(nz // 2):
            at = slice(2 * pair * BOX, (2 * pair + 2) * BOX)
            block = project(base, at)
            planes[:, at] = block if first else planes[:, at] + block

    near_first = far_first[::-1]
    add_block(block_of(y, core), True)
    across(0).wait_recv()
    add_block(block_of(y, 1 - core), False)
    for k in near_first:
        along_y(k).wait_recv()
        across(k).start()
        add_block(block_of(lax.rem(y - k + ny, ny), core), False)
        across(k).wait_recv()
        if k != near_first[-1]:
            add_block(block_of(lax.rem(y - k + ny, ny), 1 - core), False)
    final = block_of(lax.rem(y - near_first[-1] + ny, ny), 1 - core)
    reverse(final)

    def even_copy(k):
        return pltpu.make_async_remote_copy(
            give_e.at[k], take_e.at[k], s_e.at[k], r_e.at[k], device_id=at_z(k)[1], device_id_type=MESH
        )

    def odd_copy(k):
        device = ((nz - 1 - lax.rem(z + k, nz)) * nq + flip_q, slab)
        return pltpu.make_async_remote_copy(
            give_o.at[k], take_o.at[k], s_o.at[k], r_o.at[k], device_id=device, device_id_type=MESH
        )

    order = sorted(range(nz // 2), key=lambda pair: -min(2 * pair, nz - 2 * pair))
    for pair in order:
        at = slice(2 * pair * BOX, (2 * pair + 2) * BOX)
        block = planes[:, at] + project(final, at)
        for k in (2 * pair, 2 * pair + 1):
            at = (k - 2 * pair) * BOX
            give_e[k] = block[:rows, at:at + BOX].astype(BF16)
            give_o[k] = block[rows:, at:at + BOX].astype(BF16)
            odd_copy(k).start()
            if k:
                even_copy(k).start()

    for k in range(nz):
        odd_copy(k).wait()
        if k:
            even_copy(k).wait()
    for k in range(ny):
        to_core(k).wait_send()
        across(k).wait_send()
        if k:
            to_owner(k).wait_send()
            along_y(k).wait_send()
    value = give_e[0].astype(F32)
    for k in range(1, nz):
        value = value + take_e[k].astype(F32)
    out[0] = value
    value = take_o[0].astype(F32)
    for k in range(1, nz):
        value = value + take_o[k].astype(F32)
    high, rest = split(value)
    middle = (value - high.astype(F32)).astype(BF16)
    lowest = (value - high.astype(F32) - middle.astype(F32)).astype(BF16)
    out[1] = dot(jnp.concatenate([high, middle, lowest], axis=1), jnp.concatenate([mirror] * 3, axis=0))


def body(nz, nq, ns, images, projections, regions, offsets, defocus, counts, tilt_angle):
    rows = BOX // ns
    pairs = rows // 2
    ny = nq // 2
    vmem = pl.BlockSpec(memory_space=pltpu.VMEM)
    dma = pltpu.SemaphoreType.DMA
    scratch = [
        pltpu.VMEM((PART, BOX, BOX), BF16),
        pltpu.VMEM((BINS, rows, BOX), BF16),
        pltpu.VMEM((BOX, 2 * BOX), BF16),
        pltpu.VMEM((BOX, 3 * BOX), BF16),
        pltpu.VMEM((3 * BOX, BOX), BF16),
        pltpu.VMEM((BOX + rows, BOX), F32),
        pltpu.VMEM((4, PART, BOX), F32),
        pltpu.VMEM((PART * rows, BOX), F32),
        pltpu.VMEM((PART * rows, BOX), F32),
        pltpu.VMEM((nz, rows, PART, BOX), BF16),
        pltpu.VMEM((nq, pairs, 2 * BINS, BOX), BF16),
        pltpu.VMEM((nq, 24, BOX), F32),
        pltpu.VMEM((nz, 8, BOX), jnp.int32),
        pltpu.VMEM((ns, 2 * BINS, nz * PART), F32),
        pltpu.VMEM((nz, 8, BOX), F32),
        pltpu.VMEM((2, ny, rows, BINS, BOX), F32),
        pltpu.VMEM((ny, rows, BINS, BOX), F32),
        pltpu.VMEM((ny, pairs, 2 * BINS, BOX), BF16),
        pltpu.VMEM((ny, pairs, 2 * BINS, BOX), BF16),
        pltpu.VMEM((rows * BINS, BOX), F32),
        pltpu.VMEM((2 * rows, nq * BINS * BOX), BF16),
        pltpu.VMEM((nq * BINS * BOX, nz * BOX), BF16),
        pltpu.VMEM((2 * rows, nz * BOX), F32),
        pltpu.VMEM((nz, rows, BOX), BF16),
        pltpu.VMEM((nz, rows, BOX), BF16),
        pltpu.VMEM((nz, rows, BOX), BF16),
        pltpu.VMEM((nz, rows, BOX), BF16),
    ]
    scratch.append(dma((6,)))
    steps = PIECES * (nz - 1) // 2
    for count in (nq, nq, nz, steps, steps, ns, nz, ny, ny, ny, ny, nz, nz):
        scratch += [dma((count,)), dma((count,))]
    return pl.pallas_call(
        functools.partial(kernel, nz, nq, ns),
        out_shape=jax.ShapeDtypeStruct((2, rows, BOX), F32),
        in_specs=[pl.BlockSpec(memory_space=pltpu.SMEM)] * 5 + [pl.BlockSpec(memory_space=pl.ANY)] * 6,
        out_specs=vmem,
        scratch_shapes=scratch,
        compiler_params=pltpu.CompilerParams(
            collective_id=0, has_side_effects=True, vmem_limit_bytes=60 * 1024 * 1024
        ),
    )(regions, offsets, defocus, counts, tilt_angle, images, projections, *(jnp.asarray(table) for table in tables(rows)))


def solution(mesh):
    nq = PLANE_GROUP
    nz = mesh.shape["bins"] // nq
    ns = mesh.shape["slab"]
    in_specs = (
        P("bins", None, None),
        P("bins", None, None),
        P("bins", None),
        P(None, "bins"),
        P("bins"),
        P("bins"),
        P("bins"),
    )
    return jax.shard_map(
        functools.partial(body, nz, nq, ns),
        mesh=mesh,
        in_specs=in_specs,
        out_specs=P("bins", "slab", None),
        check_vma=False,
    )
```

```python
import functools

import jax
import jax.numpy as jnp
import ml_dtypes
import numpy as np
from jax import lax
from jax.experimental import pallas as pl
from jax.experimental.pallas import tpu as pltpu
from jax.sharding import PartitionSpec as P

AMP_COS = 0.1
AMP_SIN = 0.99498743710662
CHI_SCALE = 100.0
ENVELOPE = 8.0
BOX = 128
PART = 16
BINS = 8
PLANE_GROUP = 8
PIECES = 4
MESH = pl.DeviceIdType.MESH
F32 = jnp.float32
BF16 = jnp.bfloat16


def cosine_table():
    i = np.arange(BOX)
    cosine = np.cos(2.0 * np.pi / BOX * (i[:, None] * i[None, :] % BOX))
    high = cosine.astype(ml_dtypes.bfloat16)
    low = (cosine - high.astype(np.float64)).astype(ml_dtypes.bfloat16)
    return np.concatenate([high, high, low], axis=0)


def split(value):
    high = value.astype(BF16)
    return high, (value - high.astype(F32)).astype(BF16)


def dot(a, b):
    return jnp.dot(a, b, preferred_element_type=F32)


def dot_nt(a, b):
    return lax.dot_general(a, b, (((1,), (1,)), ((), ())), preferred_element_type=F32)


def kernel(
    nz, nq, ns,
    regions, offs, defocus, counts, tilt, images_hbm, proj_hbm, table_hbm,
    out,
    imgs, proj, table, taps, staged, frames, refs, meta_p, meta_z, partial, stats, share, from_core, send_y, from_y, total,
    aver, weights, planes, give_e, give_o, take_e, take_o,
    s_in, s_mp, r_mp, s_pr, r_pr, s_mz, r_mz, s_rt, r_rt, s_lf, r_lf, s_x, r_x, s_st, r_st,
    s_rc, r_rc, s_ry, r_ry, s_ac, r_ac, s_ay, r_ay, s_e, r_e, s_o, r_o,
):
    rows = BOX // ns
    pairs = rows // 2
    ny = nq // 2
    quarter = rows // PIECES
    depth = 2 * nz * nq
    me = lax.axis_index("bins")
    slab = lax.axis_index("slab")
    z = me // nq
    q = lax.rem(me, nq)
    flip_q = nq - 1 - q
    y = q // 2
    core = lax.rem(q, 2)
    other_core = (z * nq + 2 * y + 1 - core, slab)
    centre = (BOX - 1) / 2.0

    def at_q(k):
        other = lax.rem(q + k, nq)
        return other, (z * nq + other, slab)

    def at_z(k):
        other = lax.rem(z + k, nz)
        return other, (other * nq + q, slab)

    def at_y(k):
        other = lax.rem(y + k, ny)
        return other, (z * nq + 2 * other + core, slab)

    first_row = pl.multiple_of(slab * rows, rows)
    loads = [
        pltpu.make_async_copy(src, dst, s_in.at[i])
        for i, (src, dst) in enumerate(
            (
                (table_hbm, table),
                (images_hbm, imgs),
                (proj_hbm.at[:, pl.ds(first_row, rows)], proj),
            )
        )
    ]
    for load in loads:
        load.start()

    barrier = pltpu.get_barrier_semaphore()
    partners = [at_q(k)[1] for k in range(1, nq)] + [at_z(k)[1] for k in range(1, nz)]
    partners += [(lax.rem(z + k, nz) * nq + flip_q, slab) for k in range(1, nz)]
    partners += [(me, lax.rem(slab + k, ns)) for k in range(1, ns)]
    for device in partners:
        pl.semaphore_signal(barrier, inc=1, device_id=device, device_id_type=MESH)

    lane = lax.broadcasted_iota(jnp.int32, (8, BOX), 1)
    line = lax.broadcasted_iota(jnp.int32, (8, BOX), 0)
    angle = jnp.zeros((8, BOX), F32)
    count = jnp.zeros((8, BOX), jnp.int32)
    for g in range(BINS):
        angle = jnp.where(line == g, tilt[g], angle)
        count = jnp.where(line == g, counts[g], count)
    meta_p[q, 0:8, :] = jnp.log(1.0 + count.astype(F32))
    meta_p[q, 8:16, :] = jnp.cos(angle)
    meta_p[q, 16:24, :] = jnp.sin(angle)
    named = jnp.zeros((8, BOX), jnp.int32)
    for p in range(PART):
        for t in range(2):
            named = jnp.where((lane == z * PART + p) & (line == t), regions[t, p], named)
    meta_z[z] = named

    index = lax.broadcasted_iota(jnp.int32, (PART, BOX), 1)
    which = lax.broadcasted_iota(jnp.int32, (PART, BOX), 0)
    blur = jnp.zeros((PART, BOX), F32)
    for p in range(PART):
        blur = jnp.where(which == p, defocus[p], blur)
    freq = jnp.where(index < BOX // 2, index, index - BOX).astype(F32) / BOX
    square = freq * freq
    phase = CHI_SCALE * blur * square
    fade = jnp.exp(-ENVELOPE * square)
    sine, cosine = jnp.sin(phase), jnp.cos(phase)
    gains = jnp.concatenate(
        [
            -fade * (AMP_SIN * sine + AMP_COS * cosine),
            -fade * (AMP_SIN * cosine - AMP_COS * sine),
            fade * cosine,
            fade * sine,
        ],
        axis=0,
    )
    gh, gl = split(gains * (1.0 / BOX))
    loads[0].wait()
    found = dot(jnp.concatenate([gh, gl, gh], axis=1), table[...])
    for k in range(8):
        taps[pl.ds(k, 4 * PART, stride=8), :] = pltpu.roll(found, k, 1) if k else found

    loads[2].wait()
    for g in range(BINS):
        staged[g * rows:(g + 1) * rows, :] = proj[g].astype(F32)
    for r in range(pairs):
        even = staged[pl.ds(2 * r, BINS, stride=rows), :]
        odd = staged[pl.ds(2 * r + 1, BINS, stride=rows), :]
        refs[q, r] = jnp.concatenate([even, odd], axis=0).astype(BF16)

    def circulant(index, count, shift):
        eight = taps[pl.ds(pl.multiple_of(index * 8, 8), 8), :]
        return [pltpu.roll(eight, lax.rem(shift + 8 * k, BOX), 1) for k in range(count // 8)]

    def filter_one(p):
        down = lax.rem(slab * rows - offs[0, p] + 2 * BOX, BOX)
        along = lax.rem(offs[1, p] + BOX, BOX)
        left = jnp.concatenate(circulant(p, rows, down) + circulant(PART + p, rows, down), axis=0)
        t = dot(jnp.concatenate(split(left), axis=0), imgs[p])
        t = t[:2 * rows] + t[2 * rows:]
        t = jnp.concatenate([t[:rows], t[rows:]], axis=1)
        right = circulant(2 * PART + p, BOX, along) + circulant(3 * PART + p, BOX, along)
        right = jnp.concatenate(right, axis=0)
        out = dot(jnp.concatenate(split(t), axis=0), jnp.concatenate(split(right), axis=1))
        out = out[:, :BOX] + out[:, BOX:]
        staged[pl.ds(pl.multiple_of(p * rows, rows), rows), :] = out[:rows] + out[rows:]

    def filter_some(step, carry):
        for k in range(8):
            filter_one(step * 8 + k)
        return carry

    loads[1].wait()
    lax.fori_loop(0, PART // 8, filter_some, 0)
    for r in range(rows):
        frames[z, r] = staged[pl.ds(r, PART, stride=rows), :].astype(BF16)

    pl.semaphore_wait(barrier, len(partners))

    def to_q(buf, send, recv, k):
        device = at_q(k)[1]
        return pltpu.make_async_remote_copy(buf.at[q], buf.at[q], send.at[k], recv.at[k], device_id=device, device_id_type=MESH)

    def to_z(buf, send, recv, k):
        device = at_z(k)[1]
        return pltpu.make_async_remote_copy(buf.at[z], buf.at[z], send.at[k], recv.at[k], device_id=device, device_id_type=MESH)

    def ring(step, sign, send, recv):
        source = lax.rem(z + (nz - sign * (step // PIECES)), nz)
        piece = step % PIECES if sign > 0 else PIECES - 1 - step % PIECES
        ref = frames.at[source, pl.ds(piece * quarter, quarter)]
        device = (lax.rem(z + nz + sign, nz) * nq + q, slab)
        return pltpu.make_async_remote_copy(ref, ref, send.at[step], recv.at[step], device_id=device, device_id_type=MESH)

    def right(step):
        return ring(step, 1, s_rt, r_rt)

    def left(step):
        return ring(step, -1, s_lf, r_lf)

    steps = PIECES * (nz - 1) // 2
    for step in range(PIECES):
        right(step).start()
        left(step).start()
    for k in range(1, nq):
        to_q(meta_p, s_mp, r_mp, k).start()
    for k in range(1, nz):
        to_z(meta_z, s_mz, r_mz, k).start()
    for k in range(1, nq):
        to_q(refs, s_pr, r_pr, k).start()
    for k in range(1, nq):
        to_q(meta_p, s_mp, r_mp, k).wait()

    column = lax.broadcasted_iota(jnp.int32, (1, BOX), 1).astype(F32) - centre
    height = lax.broadcasted_iota(jnp.int32, (BOX, BOX), 0).astype(F32)

    def weigh(unit):
        j = unit // 2

        def one(g, carry):
            cosr = meta_p[j, pl.ds(8 + g, 1), :]
            sinr = meta_p[j, pl.ds(16 + g, 1), :]
            base = pl.multiple_of((j * BINS + g) * BOX, BOX)
            for k in range(nz):
                plane = 2 * (lax.rem(z + k, nz) * nq + q)
                away = plane.astype(F32) - (depth - 1) / 2.0
                landing = column * cosr + away * sinr + centre
                w = jnp.maximum(0.0, 1.0 - jnp.abs(landing - height))
                weights[pl.ds(base, BOX), k * BOX:(k + 1) * BOX] = w.astype(BF16)
            return carry

        first = unit % 2 * (BINS // 2)
        lax.fori_loop(first, first + BINS // 2, one, 0)

    units = 2 * nq
    for step in range(steps):
        right(step).wait_recv()
        if step + PIECES < steps:
            right(step + PIECES).start()
        left(step).wait_recv()
        if step + PIECES < steps:
            left(step + PIECES).start()
        for unit in range(step * units // steps, (step + 1) * units // steps):
            weigh(unit)

    for k in range(1, nq):
        to_q(refs, s_pr, r_pr, k).wait()
    for k in range(1, nz):
        to_z(meta_z, s_mz, r_mz, k).wait()
    for step in range(steps):
        right(step).wait_send()
        left(step).wait_send()

    lanes = nz * PART

    def frame(r):
        return frames[:, r].reshape(lanes, BOX)

    def score(r, carry):
        even, odd = carry
        a = refs[:, r].reshape(nq * 2 * BINS, BOX)
        return even + dot_nt(a, frame(2 * r)), odd + dot_nt(a, frame(2 * r + 1))

    zero = jnp.zeros((nq * 2 * BINS, lanes), F32)
    even, odd = lax.fori_loop(0, pairs, score, (zero, zero), unroll=4)
    even = even.reshape(nq, 2, BINS, lanes)[:, 0]
    odd = odd.reshape(nq, 2, BINS, lanes)[:, 1]
    scores = even + odd

    named = meta_z[0]
    for k in range(1, nz):
        named = named + meta_z[k]
    prior = meta_p[:, 0:8, :lanes]
    held, priors = [], []
    for t in range(2):
        place = named[t:t + 1, :lanes] - z * nq
        chosen = jnp.zeros((BINS, lanes), F32)
        chance = jnp.zeros((BINS, lanes), F32)
        for j in range(nq):
            chosen = jnp.where(place == j, scores[j], chosen)
            chance = jnp.where(place == j, prior[j], chance)
        partial[slab, t * BINS:(t + 1) * BINS, :] = chosen
        priors.append(chance)
        held.append((place >= 0) & (place < nq))

    def to_x(k):
        device = (me, lax.rem(slab + k, ns))
        return pltpu.make_async_remote_copy(
            partial.at[slab], partial.at[slab], s_x.at[k], r_x.at[k], device_id=device, device_id_type=MESH
        )

    for k in range(1, ns):
        to_x(k).start()
    for k in range(1, ns):
        to_x(k).wait()
    scores = partial[0]
    for k in range(1, ns):
        scores = scores + partial[k]
    low = jnp.float32(-3.0e38)
    logits = [scores[t * BINS:(t + 1) * BINS] / BOX + priors[t] for t in range(2)]
    tops = [jnp.where(held[t], jnp.max(logits[t], axis=0, keepdims=True), low) for t in range(2)]
    top = jnp.maximum(tops[0], tops[1])
    summed = jnp.zeros((1, lanes), F32)
    for t in range(2):
        grown = jnp.exp(jnp.where(held[t], logits[t] - top, low))
        summed = summed + jnp.sum(grown, axis=0, keepdims=True)
    stats[z, 0:1, :lanes] = top
    stats[z, 1:2, :lanes] = summed
    for k in range(1, nz):
        to_z(stats, s_st, r_st, k).start()
    for k in range(1, nz):
        to_z(stats, s_st, r_st, k).wait()
    best = stats[0, 0:1, :lanes]
    for k in range(1, nz):
        best = jnp.maximum(best, stats[k, 0:1, :lanes])
    whole = jnp.zeros((1, lanes), F32)
    for k in range(nz):
        whole = whole + stats[k, 1:2, :lanes] * jnp.exp(stats[k, 0:1, :lanes] - best)
    norm = best + jnp.log(whole)
    chances = [jnp.exp(jnp.where(held[t], logits[t] - norm, low)) for t in range(2)]
    posterior = []
    for j in range(nq):
        value = jnp.zeros((BINS, lanes), F32)
        for t in range(2):
            place = named[t:t + 1, :lanes] - z * nq
            value = jnp.where(place == j, chances[t], value)
        posterior.append(value)
    posterior = jnp.concatenate(posterior, axis=0).astype(BF16)

    def average(r, carry):
        a = dot(posterior, frame(r)).reshape(ny, 2, BINS, BOX)
        share[0, :, r] = a[:, 0]
        share[1, :, r] = a[:, 1]
        return carry

    lax.fori_loop(0, rows, average, 0, unroll=8)

    def to_core(k):
        place = at_y(k)[0]
        return pltpu.make_async_remote_copy(
            share.at[1 - core, place], from_core.at[place], s_rc.at[k], r_rc.at[k],
            device_id=other_core, device_id_type=MESH,
        )

    def to_owner(k):
        return pltpu.make_async_remote_copy(
            send_y.at[k], from_y.at[k], s_ry.at[k], r_ry.at[k], device_id=at_y(k)[1], device_id_type=MESH
        )

    far_first = sorted(range(1, ny), key=lambda k: -min(k, ny - k))
    for k in far_first + [0]:
        to_core(k).start()
    for k in far_first:
        place = at_y(k)[0]
        to_core(k).wait_recv()

        def pack(r, carry):
            a = share[core, place, 2 * r] + from_core[place, 2 * r]
            b = share[core, place, 2 * r + 1] + from_core[place, 2 * r + 1]
            send_y[k, r] = jnp.concatenate([a, b], axis=0).astype(BF16)
            return carry

        lax.fori_loop(0, pairs, pack, 0, unroll=8)
        to_owner(k).start()
    to_core(0).wait_recv()
    for k in range(1, ny):
        to_owner(k).wait_recv()

    def add_up(r, carry):
        a = share[core, y, 2 * r] + from_core[y, 2 * r]
        b = share[core, y, 2 * r + 1] + from_core[y, 2 * r + 1]
        value = jnp.concatenate([a, b], axis=0)
        for k in range(1, ny):
            value = value + from_y[k, r].astype(F32)
        total[pl.ds(pl.multiple_of(r * 2 * BINS, 2 * BINS), 2 * BINS), :] = value
        return carry

    lax.fori_loop(0, pairs, add_up, 0, unroll=8)
    span = BINS * BOX
    mine = pl.multiple_of(q * span, span)
    for g in range(BINS):
        block = total[pl.ds(g, rows, stride=BINS), :].astype(BF16)
        aver[0:rows, pl.ds(pl.multiple_of(mine + g * BOX, BOX), BOX)] = block

    def block_of(place, which):
        return pl.multiple_of((2 * place + which) * span, span)

    def along_y(k):
        ref = aver.at[pl.ds(0, rows), pl.ds(mine, span)]
        return pltpu.make_async_remote_copy(ref, ref, s_ay.at[k], r_ay.at[k], device_id=at_y(k)[1], device_id_type=MESH)

    def across(k):
        ref = aver.at[pl.ds(0, rows), pl.ds(block_of(lax.rem(y - k + ny, ny), core), span)]
        return pltpu.make_async_remote_copy(ref, ref, s_ac.at[k], r_ac.at[k], device_id=other_core, device_id_type=MESH)

    for k in far_first:
        along_y(k).start()
    across(0).start()

    mirror = (
        lax.broadcasted_iota(jnp.int32, (BOX, BOX), 0) + lax.broadcasted_iota(jnp.int32, (BOX, BOX), 1) == BOX - 1
    ).astype(F32).astype(BF16)

    def reverse(base):
        tiles = [aver[0:rows, pl.ds(pl.multiple_of(base + g * BOX, BOX), BOX)] for g in range(BINS)]
        turned = dot(jnp.concatenate(tiles, axis=0), mirror).astype(BF16)
        for g in range(BINS):
            aver[rows:2 * rows, pl.ds(pl.multiple_of(base + g * BOX, BOX), BOX)] = turned[g * rows:(g + 1) * rows]

    def project(base, lanes_at):
        return dot(aver[:, pl.ds(base, span)], weights[pl.ds(base, span), lanes_at])

    def add_block(base, first):
        reverse(base)
        for pair in range(nz // 2):
            at = slice(2 * pair * BOX, (2 * pair + 2) * BOX)
            block = project(base, at)
            planes[:, at] = block if first else planes[:, at] + block

    near_first = far_first[::-1]
    add_block(block_of(y, core), True)
    across(0).wait_recv()
    add_block(block_of(y, 1 - core), False)
    for k in near_first:
        along_y(k).wait_recv()
        across(k).start()
        add_block(block_of(lax.rem(y - k + ny, ny), core), False)
        across(k).wait_recv()
        if k != near_first[-1]:
            add_block(block_of(lax.rem(y - k + ny, ny), 1 - core), False)
    final = block_of(lax.rem(y - near_first[-1] + ny, ny), 1 - core)
    reverse(final)

    def even_copy(k):
        return pltpu.make_async_remote_copy(
            give_e.at[k], take_e.at[k], s_e.at[k], r_e.at[k], device_id=at_z(k)[1], device_id_type=MESH
        )

    def odd_copy(k):
        device = ((nz - 1 - lax.rem(z + k, nz)) * nq + flip_q, slab)
        return pltpu.make_async_remote_copy(
            give_o.at[k], take_o.at[k], s_o.at[k], r_o.at[k], device_id=device, device_id_type=MESH
        )

    order = sorted(range(nz // 2), key=lambda pair: -min(2 * pair, nz - 2 * pair))
    for pair in order:
        at = slice(2 * pair * BOX, (2 * pair + 2) * BOX)
        block = planes[:, at] + project(final, at)
        for k in (2 * pair, 2 * pair + 1):
            at = (k - 2 * pair) * BOX
            give_e[k] = block[:rows, at:at + BOX].astype(BF16)
            give_o[k] = block[rows:, at:at + BOX].astype(BF16)
            odd_copy(k).start()
            if k:
                even_copy(k).start()

    for k in range(nz):
        odd_copy(k).wait()
        if k:
            even_copy(k).wait()
    for k in range(ny):
        to_core(k).wait_send()
        across(k).wait_send()
        if k:
            to_owner(k).wait_send()
            along_y(k).wait_send()
    value = give_e[0].astype(F32)
    for k in range(1, nz):
        value = value + take_e[k].astype(F32)
    out[0] = value
    value = take_o[0].astype(F32)
    for k in range(1, nz):
        value = value + take_o[k].astype(F32)
    high, rest = split(value)
    middle = (value - high.astype(F32)).astype(BF16)
    lowest = (value - high.astype(F32) - middle.astype(F32)).astype(BF16)
    out[1] = dot(jnp.concatenate([high, middle, lowest], axis=1), jnp.concatenate([mirror] * 3, axis=0))


def body(nz, nq, ns, images, projections, regions, offsets, defocus, counts, tilt_angle):
    rows = BOX // ns
    pairs = rows // 2
    ny = nq // 2
    vmem = pl.BlockSpec(memory_space=pltpu.VMEM)
    dma = pltpu.SemaphoreType.DMA
    scratch = [
        pltpu.VMEM((PART, BOX, BOX), BF16),
        pltpu.VMEM((BINS, rows, BOX), BF16),
        pltpu.VMEM((3 * BOX, BOX), BF16),
        pltpu.VMEM((4 * PART * 8, BOX), F32),
        pltpu.VMEM((PART * rows, BOX), F32),
        pltpu.VMEM((nz, rows, PART, BOX), BF16),
        pltpu.VMEM((nq, pairs, 2 * BINS, BOX), BF16),
        pltpu.VMEM((nq, 24, BOX), F32),
        pltpu.VMEM((nz, 8, BOX), jnp.int32),
        pltpu.VMEM((ns, 2 * BINS, nz * PART), F32),
        pltpu.VMEM((nz, 8, BOX), F32),
        pltpu.VMEM((2, ny, rows, BINS, BOX), F32),
        pltpu.VMEM((ny, rows, BINS, BOX), F32),
        pltpu.VMEM((ny, pairs, 2 * BINS, BOX), BF16),
        pltpu.VMEM((ny, pairs, 2 * BINS, BOX), BF16),
        pltpu.VMEM((rows * BINS, BOX), F32),
        pltpu.VMEM((2 * rows, nq * BINS * BOX), BF16),
        pltpu.VMEM((nq * BINS * BOX, nz * BOX), BF16),
        pltpu.VMEM((2 * rows, nz * BOX), F32),
        pltpu.VMEM((nz, rows, BOX), BF16),
        pltpu.VMEM((nz, rows, BOX), BF16),
        pltpu.VMEM((nz, rows, BOX), BF16),
        pltpu.VMEM((nz, rows, BOX), BF16),
    ]
    scratch.append(dma((3,)))
    steps = PIECES * (nz - 1) // 2
    for count in (nq, nq, nz, steps, steps, ns, nz, ny, ny, ny, ny, nz, nz):
        scratch += [dma((count,)), dma((count,))]
    return pl.pallas_call(
        functools.partial(kernel, nz, nq, ns),
        out_shape=jax.ShapeDtypeStruct((2, rows, BOX), F32),
        in_specs=[pl.BlockSpec(memory_space=pltpu.SMEM)] * 5 + [pl.BlockSpec(memory_space=pl.ANY)] * 3,
        out_specs=vmem,
        scratch_shapes=scratch,
        compiler_params=pltpu.CompilerParams(
            collective_id=0, has_side_effects=True, vmem_limit_bytes=60 * 1024 * 1024
        ),
    )(regions.T, offsets, defocus, counts, tilt_angle, images, projections, jnp.asarray(cosine_table()))


def solution(mesh):
    nq = PLANE_GROUP
    nz = mesh.shape["bins"] // nq
    ns = mesh.shape["slab"]
    in_specs = (
        P("bins", None, None),
        P("bins", None, None),
        P("bins", None),
        P(None, "bins"),
        P("bins"),
        P("bins"),
        P("bins"),
    )
    return jax.shard_map(
        functools.partial(body, nz, nq, ns),
        mesh=mesh,
        in_specs=in_specs,
        out_specs=P("bins", "slab", None),
        check_vma=False,
    )
```

```python
import functools

import jax
import jax.numpy as jnp
import ml_dtypes
import numpy as np
from jax import lax
from jax.experimental import pallas as pl
from jax.experimental.pallas import tpu as pltpu
from jax.sharding import PartitionSpec as P

AMP_COS = 0.1
AMP_SIN = 0.99498743710662
CHI_SCALE = 100.0
ENVELOPE = 8.0
BOX = 128
PART = 16
BINS = 8
PLANE_GROUP = 8
PIECES = 4
MESH = pl.DeviceIdType.MESH
F32 = jnp.float32
BF16 = jnp.bfloat16


def cosine_table():
    i = np.arange(BOX)
    cosine = np.cos(2.0 * np.pi / BOX * (i[:, None] * i[None, :] % BOX))
    high = cosine.astype(ml_dtypes.bfloat16)
    low = (cosine - high.astype(np.float64)).astype(ml_dtypes.bfloat16)
    return np.concatenate([high, high, low], axis=0)


def split(value):
    high = value.astype(BF16)
    return high, (value - high.astype(F32)).astype(BF16)


def dot(a, b):
    return jnp.dot(a, b, preferred_element_type=F32)


def dot_nt(a, b):
    return lax.dot_general(a, b, (((1,), (1,)), ((), ())), preferred_element_type=F32)


def kernel(
    nz, nq, ns,
    regions, offs, defocus, counts, tilt, images_hbm, proj_hbm, table_hbm,
    out,
    imgs, proj, table, taps, staged, frames, refs, meta_p, meta_z, partial, stats, share, from_core, send_y, from_y, total,
    aver, weights, planes, give_e, give_o, take_e, take_o,
    s_in, s_mp, r_mp, s_pr, r_pr, s_mz, r_mz, s_rt, r_rt, s_lf, r_lf, s_x, r_x, s_st, r_st,
    s_rc, r_rc, s_ry, r_ry, s_ac, r_ac, s_ay, r_ay, s_e, r_e, s_o, r_o,
):
    rows = BOX // ns
    pairs = rows // 2
    ny = nq // 2
    quarter = rows // PIECES
    depth = 2 * nz * nq
    me = lax.axis_index("bins")
    slab = lax.axis_index("slab")
    z = me // nq
    q = lax.rem(me, nq)
    flip_q = nq - 1 - q
    y = q // 2
    core = lax.rem(q, 2)
    other_core = (z * nq + 2 * y + 1 - core, slab)
    centre = (BOX - 1) / 2.0

    def at_q(k):
        other = lax.rem(q + k, nq)
        return other, (z * nq + other, slab)

    def at_z(k):
        other = lax.rem(z + k, nz)
        return other, (other * nq + q, slab)

    def at_y(k):
        other = lax.rem(y + k, ny)
        return other, (z * nq + 2 * other + core, slab)

    first_row = pl.multiple_of(slab * rows, rows)
    loads = [
        pltpu.make_async_copy(src, dst, s_in.at[i])
        for i, (src, dst) in enumerate(
            (
                (table_hbm, table),
                (images_hbm, imgs),
                (proj_hbm.at[:, pl.ds(first_row, rows)], proj),
            )
        )
    ]
    for load in loads:
        load.start()

    barrier = pltpu.get_barrier_semaphore()
    partners = [at_q(k)[1] for k in range(1, nq)] + [at_z(k)[1] for k in range(1, nz)]
    partners += [(lax.rem(z + k, nz) * nq + flip_q, slab) for k in range(1, nz)]
    partners += [(me, lax.rem(slab + k, ns)) for k in range(1, ns)]
    for device in partners:
        pl.semaphore_signal(barrier, inc=1, device_id=device, device_id_type=MESH)

    lane = lax.broadcasted_iota(jnp.int32, (8, BOX), 1)
    line = lax.broadcasted_iota(jnp.int32, (8, BOX), 0)
    angle = jnp.zeros((8, BOX), F32)
    count = jnp.zeros((8, BOX), jnp.int32)
    for g in range(BINS):
        angle = jnp.where(line == g, tilt[g], angle)
        count = jnp.where(line == g, counts[g], count)
    meta_p[q, 0:8, :] = jnp.log(1.0 + count.astype(F32))
    meta_p[q, 8:16, :] = jnp.cos(angle)
    meta_p[q, 16:24, :] = jnp.sin(angle)
    named = jnp.zeros((8, BOX), jnp.int32)
    for p in range(PART):
        for t in range(2):
            named = jnp.where((lane == z * PART + p) & (line == t), regions[t, p], named)
    meta_z[z] = named

    index = lax.broadcasted_iota(jnp.int32, (PART, BOX), 1)
    which = lax.broadcasted_iota(jnp.int32, (PART, BOX), 0)
    blur = jnp.zeros((PART, BOX), F32)
    for p in range(PART):
        blur = jnp.where(which == p, defocus[p], blur)
    freq = jnp.where(index < BOX // 2, index, index - BOX).astype(F32) / BOX
    square = freq * freq
    phase = CHI_SCALE * blur * square
    fade = jnp.exp(-ENVELOPE * square)
    sine, cosine = jnp.sin(phase), jnp.cos(phase)
    gains = jnp.concatenate(
        [
            -fade * (AMP_SIN * sine + AMP_COS * cosine),
            -fade * (AMP_SIN * cosine - AMP_COS * sine),
            fade * cosine,
            fade * sine,
        ],
        axis=0,
    )
    gh, gl = split(gains * (1.0 / BOX))
    loads[0].wait()
    found = dot(jnp.concatenate([gh, gl, gh], axis=1), table[...])
    for k in range(8):
        taps[pl.ds(k, 4 * PART, stride=8), :] = pltpu.roll(found, k, 1) if k else found

    loads[2].wait()
    for g in range(BINS):
        staged[g * rows:(g + 1) * rows, :] = proj[g].astype(F32)
    for r in range(pairs):
        even = staged[pl.ds(2 * r, BINS, stride=rows), :]
        odd = staged[pl.ds(2 * r + 1, BINS, stride=rows), :]
        refs[q, r] = jnp.concatenate([even, odd], axis=0).astype(BF16)

    def circulant(index, count, shift):
        eight = taps[pl.ds(pl.multiple_of(index * 8, 8), 8), :]
        return [pltpu.roll(eight, lax.rem(shift + 8 * k, BOX), 1) for k in range(count // 8)]

    def filter_one(p):
        down = lax.rem(slab * rows - offs[0, p] + 2 * BOX, BOX)
        along = lax.rem(offs[1, p] + BOX, BOX)
        left = jnp.concatenate(circulant(p, rows, down) + circulant(PART + p, rows, down), axis=0)
        t = dot(jnp.concatenate(split(left), axis=0), imgs[p])
        t = t[:2 * rows] + t[2 * rows:]
        t = jnp.concatenate([t[:rows], t[rows:]], axis=1)
        right = circulant(2 * PART + p, BOX, along) + circulant(3 * PART + p, BOX, along)
        right = jnp.concatenate(right, axis=0)
        out = dot(jnp.concatenate(split(t), axis=0), jnp.concatenate(split(right), axis=1))
        out = out[:, :BOX] + out[:, BOX:]
        staged[pl.ds(pl.multiple_of(p * rows, rows), rows), :] = out[:rows] + out[rows:]

    def filter_some(step, carry):
        for k in range(8):
            filter_one(step * 8 + k)
        return carry

    loads[1].wait()
    lax.fori_loop(0, PART // 8, filter_some, 0)
    for r in range(rows):
        frames[z, r] = staged[pl.ds(r, PART, stride=rows), :].astype(BF16)

    pl.semaphore_wait(barrier, len(partners))

    def to_q(buf, send, recv, k):
        device = at_q(k)[1]
        return pltpu.make_async_remote_copy(buf.at[q], buf.at[q], send.at[k], recv.at[k], device_id=device, device_id_type=MESH)

    def to_z(buf, send, recv, k):
        device = at_z(k)[1]
        return pltpu.make_async_remote_copy(buf.at[z], buf.at[z], send.at[k], recv.at[k], device_id=device, device_id_type=MESH)

    def ring(step, sign, send, recv):
        source = lax.rem(z + (nz - sign * (step // PIECES)), nz)
        piece = step % PIECES if sign > 0 else PIECES - 1 - step % PIECES
        ref = frames.at[source, pl.ds(piece * quarter, quarter)]
        device = (lax.rem(z + nz + sign, nz) * nq + q, slab)
        return pltpu.make_async_remote_copy(ref, ref, send.at[step], recv.at[step], device_id=device, device_id_type=MESH)

    def right(step):
        return ring(step, 1, s_rt, r_rt)

    def left(step):
        return ring(step, -1, s_lf, r_lf)

    steps = PIECES * (nz - 1) // 2
    for step in range(PIECES):
        right(step).start()
        left(step).start()
    for k in range(1, nq):
        to_q(meta_p, s_mp, r_mp, k).start()
    for k in range(1, nz):
        to_z(meta_z, s_mz, r_mz, k).start()
    for k in range(1, nq):
        to_q(refs, s_pr, r_pr, k).start()
    for k in range(1, nq):
        to_q(meta_p, s_mp, r_mp, k).wait()

    column = lax.broadcasted_iota(jnp.int32, (1, BOX), 1).astype(F32) - centre
    height = lax.broadcasted_iota(jnp.int32, (BOX, BOX), 0).astype(F32)

    def weigh(unit):
        j = unit // 2

        def one(g, carry):
            cosr = meta_p[j, pl.ds(8 + g, 1), :]
            sinr = meta_p[j, pl.ds(16 + g, 1), :]
            base = pl.multiple_of((j * BINS + g) * BOX, BOX)
            for k in range(nz):
                plane = 2 * (lax.rem(z + k, nz) * nq + q)
                away = plane.astype(F32) - (depth - 1) / 2.0
                landing = column * cosr + away * sinr + centre
                w = jnp.maximum(0.0, 1.0 - jnp.abs(landing - height))
                weights[pl.ds(base, BOX), k * BOX:(k + 1) * BOX] = w.astype(BF16)
            return carry

        first = unit % 2 * (BINS // 2)
        lax.fori_loop(first, first + BINS // 2, one, 0)

    units = 2 * nq
    for step in range(steps):
        right(step).wait_recv()
        if step + PIECES < steps:
            right(step + PIECES).start()
        left(step).wait_recv()
        if step + PIECES < steps:
            left(step + PIECES).start()
        for unit in range(step * units // steps, (step + 1) * units // steps):
            weigh(unit)

    for k in range(1, nq):
        to_q(refs, s_pr, r_pr, k).wait()
    for k in range(1, nz):
        to_z(meta_z, s_mz, r_mz, k).wait()
    for step in range(steps):
        right(step).wait_send()
        left(step).wait_send()

    lanes = nz * PART

    def frame(r):
        return frames[:, r].reshape(lanes, BOX)

    def score(r, carry):
        even, odd = carry
        a = refs[:, r].reshape(nq * 2 * BINS, BOX)
        return even + dot_nt(a, frame(2 * r)), odd + dot_nt(a, frame(2 * r + 1))

    zero = jnp.zeros((nq * 2 * BINS, lanes), F32)
    even, odd = lax.fori_loop(0, pairs, score, (zero, zero), unroll=4)
    even = even.reshape(nq, 2, BINS, lanes)[:, 0]
    odd = odd.reshape(nq, 2, BINS, lanes)[:, 1]
    scores = even + odd

    named = meta_z[0]
    for k in range(1, nz):
        named = named + meta_z[k]
    prior = meta_p[:, 0:8, :lanes]
    held, priors = [], []
    for t in range(2):
        place = named[t:t + 1, :lanes] - z * nq
        chosen = jnp.zeros((BINS, lanes), F32)
        chance = jnp.zeros((BINS, lanes), F32)
        for j in range(nq):
            chosen = jnp.where(place == j, scores[j], chosen)
            chance = jnp.where(place == j, prior[j], chance)
        partial[slab, t * BINS:(t + 1) * BINS, :] = chosen
        priors.append(chance)
        held.append((place >= 0) & (place < nq))

    def to_x(k):
        device = (me, lax.rem(slab + k, ns))
        return pltpu.make_async_remote_copy(
            partial.at[slab], partial.at[slab], s_x.at[k], r_x.at[k], device_id=device, device_id_type=MESH
        )

    for k in range(1, ns):
        to_x(k).start()
    for k in range(1, ns):
        to_x(k).wait()
    scores = partial[0]
    for k in range(1, ns):
        scores = scores + partial[k]
    low = jnp.float32(-3.0e38)
    logits = [scores[t * BINS:(t + 1) * BINS] / BOX + priors[t] for t in range(2)]
    tops = [jnp.where(held[t], jnp.max(logits[t], axis=0, keepdims=True), low) for t in range(2)]
    top = jnp.maximum(tops[0], tops[1])
    summed = jnp.zeros((1, lanes), F32)
    for t in range(2):
        grown = jnp.exp(jnp.where(held[t], logits[t] - top, low))
        summed = summed + jnp.sum(grown, axis=0, keepdims=True)
    stats[z, 0:1, :lanes] = top
    stats[z, 1:2, :lanes] = summed
    for k in range(1, nz):
        to_z(stats, s_st, r_st, k).start()
    for k in range(1, nz):
        to_z(stats, s_st, r_st, k).wait()
    best = stats[0, 0:1, :lanes]
    for k in range(1, nz):
        best = jnp.maximum(best, stats[k, 0:1, :lanes])
    whole = jnp.zeros((1, lanes), F32)
    for k in range(nz):
        whole = whole + stats[k, 1:2, :lanes] * jnp.exp(stats[k, 0:1, :lanes] - best)
    norm = best + jnp.log(whole)
    chances = [jnp.exp(jnp.where(held[t], logits[t] - norm, low)) for t in range(2)]
    posterior = []
    for j in range(nq):
        value = jnp.zeros((BINS, lanes), F32)
        for t in range(2):
            place = named[t:t + 1, :lanes] - z * nq
            value = jnp.where(place == j, chances[t], value)
        posterior.append(value)
    posterior = jnp.concatenate(posterior, axis=0).astype(BF16)

    def average(r, carry):
        a = dot(posterior, frame(r)).reshape(ny, 2, BINS, BOX)
        share[0, :, r] = a[:, 0]
        share[1, :, r] = a[:, 1]
        return carry

    half = rows // 2

    def to_core(k, h):
        place = at_y(k)[0]
        part = pl.ds(h * half, half)
        return pltpu.make_async_remote_copy(
            share.at[1 - core, place, part], from_core.at[place, part], s_rc.at[2 * k + h], r_rc.at[2 * k + h],
            device_id=other_core, device_id_type=MESH,
        )

    def to_owner(k, h):
        part = pl.ds(h * half // 2, half // 2)
        return pltpu.make_async_remote_copy(
            send_y.at[k, part], from_y.at[k, part], s_ry.at[2 * k + h], r_ry.at[2 * k + h],
            device_id=at_y(k)[1], device_id_type=MESH,
        )

    span = BINS * BOX
    mine = pl.multiple_of(q * span, span)

    def block_of(place, which):
        return pl.multiple_of((2 * place + which) * span, span)

    def along_y(k, h):
        ref = aver.at[pl.ds(h * half, half), pl.ds(mine, span)]
        return pltpu.make_async_remote_copy(
            ref, ref, s_ay.at[2 * k + h], r_ay.at[2 * k + h], device_id=at_y(k)[1], device_id_type=MESH
        )

    def across(k, h):
        ref = aver.at[pl.ds(h * half, half), pl.ds(block_of(lax.rem(y - k + ny, ny), core), span)]
        return pltpu.make_async_remote_copy(
            ref, ref, s_ac.at[2 * k + h], r_ac.at[2 * k + h], device_id=other_core, device_id_type=MESH
        )

    far_first = sorted(range(1, ny), key=lambda k: -min(k, ny - k))
    for h in range(2):
        lax.fori_loop(h * half, (h + 1) * half, average, 0, unroll=8)
        for k in far_first + [0]:
            to_core(k, h).start()
    for h in range(2):
        for k in far_first:
            place = at_y(k)[0]
            to_core(k, h).wait_recv()

            def pack(r, carry):
                a = share[core, place, 2 * r] + from_core[place, 2 * r]
                b = share[core, place, 2 * r + 1] + from_core[place, 2 * r + 1]
                send_y[k, r] = jnp.concatenate([a, b], axis=0).astype(BF16)
                return carry

            lax.fori_loop(h * half // 2, (h + 1) * half // 2, pack, 0, unroll=8)
            to_owner(k, h).start()

    def add_up(r, carry):
        a = share[core, y, 2 * r] + from_core[y, 2 * r]
        b = share[core, y, 2 * r + 1] + from_core[y, 2 * r + 1]
        value = jnp.concatenate([a, b], axis=0)
        for k in range(1, ny):
            value = value + from_y[k, r].astype(F32)
        total[pl.ds(pl.multiple_of(r * 2 * BINS, 2 * BINS), 2 * BINS), :] = value
        return carry

    for h in range(2):
        to_core(0, h).wait_recv()
        for k in far_first[::-1]:
            to_owner(k, h).wait_recv()
        lax.fori_loop(h * half // 2, (h + 1) * half // 2, add_up, 0, unroll=8)
        for g in range(BINS):
            block = total[pl.ds(h * half * BINS + g, half, stride=BINS), :].astype(BF16)
            aver[h * half:(h + 1) * half, pl.ds(pl.multiple_of(mine + g * BOX, BOX), BOX)] = block
        for k in far_first:
            along_y(k, h).start()
        across(0, h).start()

    mirror = (
        lax.broadcasted_iota(jnp.int32, (BOX, BOX), 0) + lax.broadcasted_iota(jnp.int32, (BOX, BOX), 1) == BOX - 1
    ).astype(F32).astype(BF16)

    def reverse(base):
        tiles = [aver[0:rows, pl.ds(pl.multiple_of(base + g * BOX, BOX), BOX)] for g in range(BINS)]
        turned = dot(jnp.concatenate(tiles, axis=0), mirror).astype(BF16)
        for g in range(BINS):
            aver[rows:2 * rows, pl.ds(pl.multiple_of(base + g * BOX, BOX), BOX)] = turned[g * rows:(g + 1) * rows]

    def project(base, lanes_at):
        return dot(aver[:, pl.ds(base, span)], weights[pl.ds(base, span), lanes_at])

    def add_block(base, first):
        reverse(base)
        for pair in range(nz // 2):
            at = slice(2 * pair * BOX, (2 * pair + 2) * BOX)
            block = project(base, at)
            planes[:, at] = block if first else planes[:, at] + block

    def back(k, which):
        return block_of(lax.rem(y - k + ny, ny), which)

    near_first = far_first[::-1]
    add_block(back(0, core), True)
    for h in range(2):
        across(0, h).wait_recv()
    add_block(back(0, 1 - core), False)
    for k in near_first:
        along_y(k, 0).wait_recv()
        across(k, 0).start()
    for k in near_first:
        along_y(k, 1).wait_recv()
        across(k, 1).start()
        add_block(back(k, core), False)
    for k in near_first:
        for h in range(2):
            across(k, h).wait_recv()
        if k != near_first[-1]:
            add_block(back(k, 1 - core), False)
    final = back(near_first[-1], 1 - core)
    reverse(final)

    def even_copy(k):
        return pltpu.make_async_remote_copy(
            give_e.at[k], take_e.at[k], s_e.at[k], r_e.at[k], device_id=at_z(k)[1], device_id_type=MESH
        )

    def odd_copy(k):
        device = ((nz - 1 - lax.rem(z + k, nz)) * nq + flip_q, slab)
        return pltpu.make_async_remote_copy(
            give_o.at[k], take_o.at[k], s_o.at[k], r_o.at[k], device_id=device, device_id_type=MESH
        )

    order = sorted(range(nz // 2), key=lambda pair: -min(2 * pair, nz - 2 * pair))
    for pair in order:
        at = slice(2 * pair * BOX, (2 * pair + 2) * BOX)
        block = planes[:, at] + project(final, at)
        for k in (2 * pair, 2 * pair + 1):
            at = (k - 2 * pair) * BOX
            give_e[k] = block[:rows, at:at + BOX].astype(BF16)
            give_o[k] = block[rows:, at:at + BOX].astype(BF16)
            odd_copy(k).start()
            if k:
                even_copy(k).start()

    for k in range(nz):
        odd_copy(k).wait()
        if k:
            even_copy(k).wait()
    for k in range(ny):
        for h in range(2):
            to_core(k, h).wait_send()
            across(k, h).wait_send()
            if k:
                to_owner(k, h).wait_send()
                along_y(k, h).wait_send()
    value = give_e[0].astype(F32)
    for k in range(1, nz):
        value = value + take_e[k].astype(F32)
    out[0] = value
    value = take_o[0].astype(F32)
    for k in range(1, nz):
        value = value + take_o[k].astype(F32)
    high, rest = split(value)
    middle = (value - high.astype(F32)).astype(BF16)
    lowest = (value - high.astype(F32) - middle.astype(F32)).astype(BF16)
    out[1] = dot(jnp.concatenate([high, middle, lowest], axis=1), jnp.concatenate([mirror] * 3, axis=0))


def body(nz, nq, ns, images, projections, regions, offsets, defocus, counts, tilt_angle):
    rows = BOX // ns
    pairs = rows // 2
    ny = nq // 2
    vmem = pl.BlockSpec(memory_space=pltpu.VMEM)
    dma = pltpu.SemaphoreType.DMA
    scratch = [
        pltpu.VMEM((PART, BOX, BOX), BF16),
        pltpu.VMEM((BINS, rows, BOX), BF16),
        pltpu.VMEM((3 * BOX, BOX), BF16),
        pltpu.VMEM((4 * PART * 8, BOX), F32),
        pltpu.VMEM((PART * rows, BOX), F32),
        pltpu.VMEM((nz, rows, PART, BOX), BF16),
        pltpu.VMEM((nq, pairs, 2 * BINS, BOX), BF16),
        pltpu.VMEM((nq, 24, BOX), F32),
        pltpu.VMEM((nz, 8, BOX), jnp.int32),
        pltpu.VMEM((ns, 2 * BINS, nz * PART), F32),
        pltpu.VMEM((nz, 8, BOX), F32),
        pltpu.VMEM((2, ny, rows, BINS, BOX), F32),
        pltpu.VMEM((ny, rows, BINS, BOX), F32),
        pltpu.VMEM((ny, pairs, 2 * BINS, BOX), BF16),
        pltpu.VMEM((ny, pairs, 2 * BINS, BOX), BF16),
        pltpu.VMEM((rows * BINS, BOX), F32),
        pltpu.VMEM((2 * rows, nq * BINS * BOX), BF16),
        pltpu.VMEM((nq * BINS * BOX, nz * BOX), BF16),
        pltpu.VMEM((2 * rows, nz * BOX), F32),
        pltpu.VMEM((nz, rows, BOX), BF16),
        pltpu.VMEM((nz, rows, BOX), BF16),
        pltpu.VMEM((nz, rows, BOX), BF16),
        pltpu.VMEM((nz, rows, BOX), BF16),
    ]
    scratch.append(dma((3,)))
    steps = PIECES * (nz - 1) // 2
    for count in (nq, nq, nz, steps, steps, ns, nz, 2 * ny, 2 * ny, 2 * ny, 2 * ny, nz, nz):
        scratch += [dma((count,)), dma((count,))]
    return pl.pallas_call(
        functools.partial(kernel, nz, nq, ns),
        out_shape=pltpu.VMEM((2, rows, BOX), F32),
        in_specs=[pl.BlockSpec(memory_space=pltpu.SMEM)] * 5 + [pl.BlockSpec(memory_space=pl.ANY)] * 3,
        out_specs=vmem,
        scratch_shapes=scratch,
        compiler_params=pltpu.CompilerParams(
            collective_id=0, has_side_effects=True, vmem_limit_bytes=60 * 1024 * 1024
        ),
    )(regions.T, offsets, defocus, counts, tilt_angle, images, projections, jnp.asarray(cosine_table()))


def solution(mesh):
    nq = PLANE_GROUP
    nz = mesh.shape["bins"] // nq
    ns = mesh.shape["slab"]
    in_specs = (
        P("bins", None, None),
        P("bins", None, None),
        P("bins", None),
        P(None, "bins"),
        P("bins"),
        P("bins"),
        P("bins"),
    )
    return jax.shard_map(
        functools.partial(body, nz, nq, ns),
        mesh=mesh,
        in_specs=in_specs,
        out_specs=P("bins", "slab", None),
        check_vma=False,
    )
```

```python
import functools

import jax
import jax.numpy as jnp
import ml_dtypes
import numpy as np
from jax import lax
from jax.experimental import pallas as pl
from jax.experimental.pallas import tpu as pltpu
from jax.sharding import PartitionSpec as P

AMP_COS = 0.1
AMP_SIN = 0.99498743710662
CHI_SCALE = 100.0
ENVELOPE = 8.0
BOX = 128
PART = 16
BINS = 8
PLANE_GROUP = 8
PIECES = 4
MESH = pl.DeviceIdType.MESH
F32 = jnp.float32
BF16 = jnp.bfloat16


def cosine_table():
    i = np.arange(BOX)
    cosine = np.cos(2.0 * np.pi / BOX * (i[:, None] * i[None, :] % BOX))
    high = cosine.astype(ml_dtypes.bfloat16)
    low = (cosine - high.astype(np.float64)).astype(ml_dtypes.bfloat16)
    return np.concatenate([high, high, low], axis=0)


def split(value):
    high = value.astype(BF16)
    return high, (value - high.astype(F32)).astype(BF16)


def dot(a, b):
    return jnp.dot(a, b, preferred_element_type=F32)


def dot_nt(a, b):
    return lax.dot_general(a, b, (((1,), (1,)), ((), ())), preferred_element_type=F32)


def kernel(
    nz, nq, ns,
    regions, offs, defocus, counts, tilt, images_hbm, proj_hbm, table_hbm,
    out,
    imgs, proj, table, taps, staged, frames, refs, meta_p, meta_z, partial, stats, share, from_core, send_y, from_y, total,
    aver, weights, planes, give_e, give_o, take_e, take_o,
    s_in, s_mp, r_mp, s_pr, r_pr, s_mz, r_mz, s_rt, r_rt, s_lf, r_lf, s_x, r_x, s_st, r_st,
    s_rc, r_rc, s_ry, r_ry, s_ac, r_ac, s_ay, r_ay, s_e, r_e, s_o, r_o,
):
    rows = BOX // ns
    pairs = rows // 2
    ny = nq // 2
    quarter = rows // PIECES
    depth = 2 * nz * nq
    me = lax.axis_index("bins")
    slab = lax.axis_index("slab")
    z = me // nq
    q = lax.rem(me, nq)
    flip_q = nq - 1 - q
    y = q // 2
    core = lax.rem(q, 2)
    other_core = (z * nq + 2 * y + 1 - core, slab)
    centre = (BOX - 1) / 2.0

    def at_q(k):
        other = lax.rem(q + k, nq)
        return other, (z * nq + other, slab)

    def at_z(k):
        other = lax.rem(z + k, nz)
        return other, (other * nq + q, slab)

    def at_y(k):
        other = lax.rem(y + k, ny)
        return other, (z * nq + 2 * other + core, slab)

    first_row = pl.multiple_of(slab * rows, rows)
    loads = [
        pltpu.make_async_copy(src, dst, s_in.at[i])
        for i, (src, dst) in enumerate(
            (
                (table_hbm, table),
                (images_hbm, imgs),
                (proj_hbm.at[:, pl.ds(first_row, rows)], proj),
            )
        )
    ]
    for load in loads:
        load.start()

    barrier = pltpu.get_barrier_semaphore()
    partners = [at_q(k)[1] for k in range(1, nq)] + [at_z(k)[1] for k in range(1, nz)]
    partners += [(lax.rem(z + k, nz) * nq + flip_q, slab) for k in range(1, nz)]
    partners += [(me, lax.rem(slab + k, ns)) for k in range(1, ns)]
    for device in partners:
        pl.semaphore_signal(barrier, inc=1, device_id=device, device_id_type=MESH)

    lane = lax.broadcasted_iota(jnp.int32, (8, BOX), 1)
    line = lax.broadcasted_iota(jnp.int32, (8, BOX), 0)
    angle = jnp.zeros((8, BOX), F32)
    count = jnp.zeros((8, BOX), jnp.int32)
    for g in range(BINS):
        angle = jnp.where(line == g, tilt[g], angle)
        count = jnp.where(line == g, counts[g], count)
    meta_p[q, 0:8, :] = jnp.log(1.0 + count.astype(F32))
    meta_p[q, 8:16, :] = jnp.cos(angle)
    meta_p[q, 16:24, :] = jnp.sin(angle)
    named = jnp.zeros((8, BOX), jnp.int32)
    for p in range(PART):
        for t in range(2):
            named = jnp.where((lane == z * PART + p) & (line == t), regions[t, p], named)
    meta_z[z] = named

    index = lax.broadcasted_iota(jnp.int32, (PART, BOX), 1)
    which = lax.broadcasted_iota(jnp.int32, (PART, BOX), 0)
    blur = jnp.zeros((PART, BOX), F32)
    for p in range(PART):
        blur = jnp.where(which == p, defocus[p], blur)
    freq = jnp.where(index < BOX // 2, index, index - BOX).astype(F32) / BOX
    square = freq * freq
    phase = CHI_SCALE * blur * square
    fade = jnp.exp(-ENVELOPE * square)
    sine, cosine = jnp.sin(phase), jnp.cos(phase)
    gains = jnp.concatenate(
        [
            -fade * (AMP_SIN * sine + AMP_COS * cosine),
            -fade * (AMP_SIN * cosine - AMP_COS * sine),
            fade * cosine,
            fade * sine,
        ],
        axis=0,
    )
    gh, gl = split(gains * (1.0 / BOX))
    loads[0].wait()
    found = dot(jnp.concatenate([gh, gl, gh], axis=1), table[...])
    for k in range(8):
        taps[pl.ds(k, 4 * PART, stride=8), :] = pltpu.roll(found, k, 1) if k else found

    loads[2].wait()
    for g in range(BINS):
        staged[g * rows:(g + 1) * rows, :] = proj[g].astype(F32)
    for r in range(rows // 4):
        lines = [staged[pl.ds(4 * r + k, BINS, stride=rows), :] for k in range(4)]
        upper, lower = jnp.concatenate(lines[:2], axis=1), jnp.concatenate(lines[2:], axis=1)
        refs[q, r] = jnp.concatenate([upper, lower], axis=0).astype(BF16)

    def circulant(index, count, shift):
        eight = taps[pl.ds(pl.multiple_of(index * 8, 8), 8), :]
        return [pltpu.roll(eight, lax.rem(shift + 8 * k, BOX), 1) for k in range(count // 8)]

    def filter_one(p):
        down = lax.rem(slab * rows - offs[0, p] + 2 * BOX, BOX)
        along = lax.rem(offs[1, p] + BOX, BOX)
        left = jnp.concatenate(circulant(p, rows, down) + circulant(PART + p, rows, down), axis=0)
        t = dot(jnp.concatenate(split(left), axis=0), imgs[p])
        t = t[:2 * rows] + t[2 * rows:]
        t = jnp.concatenate([t[:rows], t[rows:]], axis=1)
        right = circulant(2 * PART + p, BOX, along) + circulant(3 * PART + p, BOX, along)
        right = jnp.concatenate(right, axis=0)
        out = dot(jnp.concatenate(split(t), axis=0), jnp.concatenate(split(right), axis=1))
        out = out[:, :BOX] + out[:, BOX:]
        staged[pl.ds(pl.multiple_of(p * rows, rows), rows), :] = out[:rows] + out[rows:]

    def filter_some(step, carry):
        for k in range(8):
            filter_one(step * 8 + k)
        return carry

    loads[1].wait()
    lax.fori_loop(0, PART // 8, filter_some, 0)
    for r in range(rows):
        frames[z, r] = staged[pl.ds(r, PART, stride=rows), :].astype(BF16)

    pl.semaphore_wait(barrier, len(partners))

    def to_q(buf, send, recv, k):
        device = at_q(k)[1]
        return pltpu.make_async_remote_copy(buf.at[q], buf.at[q], send.at[k], recv.at[k], device_id=device, device_id_type=MESH)

    def to_z(buf, send, recv, k):
        device = at_z(k)[1]
        return pltpu.make_async_remote_copy(buf.at[z], buf.at[z], send.at[k], recv.at[k], device_id=device, device_id_type=MESH)

    def ring(step, sign, send, recv):
        source = lax.rem(z + (nz - sign * (step // PIECES)), nz)
        piece = step % PIECES if sign > 0 else PIECES - 1 - step % PIECES
        ref = frames.at[source, pl.ds(piece * quarter, quarter)]
        device = (lax.rem(z + nz + sign, nz) * nq + q, slab)
        return pltpu.make_async_remote_copy(ref, ref, send.at[step], recv.at[step], device_id=device, device_id_type=MESH)

    def right(step):
        return ring(step, 1, s_rt, r_rt)

    def left(step):
        return ring(step, -1, s_lf, r_lf)

    steps = PIECES * (nz - 1) // 2
    for step in range(PIECES):
        right(step).start()
        left(step).start()
    for k in range(1, nq):
        to_q(meta_p, s_mp, r_mp, k).start()
    for k in range(1, nz):
        to_z(meta_z, s_mz, r_mz, k).start()
    for k in range(1, nq):
        to_q(refs, s_pr, r_pr, k).start()
    for k in range(1, nq):
        to_q(meta_p, s_mp, r_mp, k).wait()

    column = lax.broadcasted_iota(jnp.int32, (1, BOX), 1).astype(F32) - centre
    height = lax.broadcasted_iota(jnp.int32, (BOX, BOX), 0).astype(F32)

    def weigh(unit):
        j = unit // 2

        def one(g, carry):
            cosr = meta_p[j, pl.ds(8 + g, 1), :]
            sinr = meta_p[j, pl.ds(16 + g, 1), :]
            base = pl.multiple_of((j * BINS + g) * BOX, BOX)
            for k in range(nz):
                plane = 2 * (lax.rem(z + k, nz) * nq + q)
                away = plane.astype(F32) - (depth - 1) / 2.0
                landing = column * cosr + away * sinr + centre
                w = jnp.maximum(0.0, 1.0 - jnp.abs(landing - height))
                weights[pl.ds(base, BOX), k * BOX:(k + 1) * BOX] = w.astype(BF16)
            return carry

        first = unit % 2 * (BINS // 2)
        lax.fori_loop(first, first + BINS // 2, one, 0)

    units = 2 * nq
    for step in range(steps):
        right(step).wait_recv()
        if step + PIECES < steps:
            right(step + PIECES).start()
        left(step).wait_recv()
        if step + PIECES < steps:
            left(step + PIECES).start()

    for k in range(1, nq):
        to_q(refs, s_pr, r_pr, k).wait()
    for k in range(1, nz):
        to_z(meta_z, s_mz, r_mz, k).wait()
    for step in range(steps):
        right(step).wait_send()
        left(step).wait_send()

    lanes = nz * PART

    def frame(r):
        return frames[:, r].reshape(lanes, BOX)

    def frame_pair(r):
        return jnp.concatenate([frame(2 * r), frame(2 * r + 1)], axis=1)

    def score(r, found):
        a = refs[:, r].reshape(nq * 2 * BINS, 2 * BOX)
        return found + dot_nt(a, jnp.concatenate([frame_pair(2 * r), frame_pair(2 * r + 1)], axis=0))

    found = jnp.zeros((nq * 2 * BINS, 2 * lanes), F32)
    found = lax.fori_loop(0, rows // 4, score, found, unroll=4).reshape(nq, 2, BINS, 2 * lanes)
    scores = found[:, 0, :, :lanes] + found[:, 1, :, lanes:]

    named = meta_z[0]
    for k in range(1, nz):
        named = named + meta_z[k]
    prior = meta_p[:, 0:8, :lanes]
    held, priors = [], []
    for t in range(2):
        place = named[t:t + 1, :lanes] - z * nq
        chosen = jnp.zeros((BINS, lanes), F32)
        chance = jnp.zeros((BINS, lanes), F32)
        for j in range(nq):
            chosen = jnp.where(place == j, scores[j], chosen)
            chance = jnp.where(place == j, prior[j], chance)
        partial[slab, t * BINS:(t + 1) * BINS, :] = chosen
        priors.append(chance)
        held.append((place >= 0) & (place < nq))

    def to_x(k):
        device = (me, lax.rem(slab + k, ns))
        return pltpu.make_async_remote_copy(
            partial.at[slab], partial.at[slab], s_x.at[k], r_x.at[k], device_id=device, device_id_type=MESH
        )

    for k in range(1, ns):
        to_x(k).start()
    for unit in range(units // 3):
        weigh(unit)
    for k in range(1, ns):
        to_x(k).wait()
    scores = partial[0]
    for k in range(1, ns):
        scores = scores + partial[k]
    low = jnp.float32(-3.0e38)
    logits = [scores[t * BINS:(t + 1) * BINS] / BOX + priors[t] for t in range(2)]
    tops = [jnp.where(held[t], jnp.max(logits[t], axis=0, keepdims=True), low) for t in range(2)]
    top = jnp.maximum(tops[0], tops[1])
    summed = jnp.zeros((1, lanes), F32)
    for t in range(2):
        grown = jnp.exp(jnp.where(held[t], logits[t] - top, low))
        summed = summed + jnp.sum(grown, axis=0, keepdims=True)
    stats[z, 0:1, :lanes] = top
    stats[z, 1:2, :lanes] = summed
    for k in range(1, nz):
        to_z(stats, s_st, r_st, k).start()
    for unit in range(units // 3, units):
        weigh(unit)
    for k in range(1, nz):
        to_z(stats, s_st, r_st, k).wait()
    best = stats[0, 0:1, :lanes]
    for k in range(1, nz):
        best = jnp.maximum(best, stats[k, 0:1, :lanes])
    whole = jnp.zeros((1, lanes), F32)
    for k in range(nz):
        whole = whole + stats[k, 1:2, :lanes] * jnp.exp(stats[k, 0:1, :lanes] - best)
    norm = best + jnp.log(whole)
    chances = [jnp.exp(jnp.where(held[t], logits[t] - norm, low)) for t in range(2)]
    posterior = []
    for j in range(nq):
        value = jnp.zeros((BINS, lanes), F32)
        for t in range(2):
            place = named[t:t + 1, :lanes] - z * nq
            value = jnp.where(place == j, chances[t], value)
        posterior.append(value)
    posterior = jnp.concatenate(posterior, axis=0).astype(BF16)

    def average(r, carry):
        a = dot(posterior, frame_pair(r)).reshape(ny, 2, BINS, 2 * BOX)
        for which in range(2):
            share[which, :, 2 * r] = a[:, which, :, :BOX]
            share[which, :, 2 * r + 1] = a[:, which, :, BOX:]
        return carry

    half = rows // 2

    def to_core(k, h):
        place = at_y(k)[0]
        part = pl.ds(h * half, half)
        return pltpu.make_async_remote_copy(
            share.at[1 - core, place, part], from_core.at[place, part], s_rc.at[2 * k + h], r_rc.at[2 * k + h],
            device_id=other_core, device_id_type=MESH,
        )

    def to_owner(k, h):
        part = pl.ds(h * half // 2, half // 2)
        return pltpu.make_async_remote_copy(
            send_y.at[k, part], from_y.at[k, part], s_ry.at[2 * k + h], r_ry.at[2 * k + h],
            device_id=at_y(k)[1], device_id_type=MESH,
        )

    span = BINS * BOX
    mine = pl.multiple_of(q * span, span)

    def block_of(place, which):
        return pl.multiple_of((2 * place + which) * span, span)

    def along_y(k, h):
        ref = aver.at[pl.ds(h * half, half), pl.ds(mine, span)]
        return pltpu.make_async_remote_copy(
            ref, ref, s_ay.at[2 * k + h], r_ay.at[2 * k + h], device_id=at_y(k)[1], device_id_type=MESH
        )

    def across(k, h):
        ref = aver.at[pl.ds(h * half, half), pl.ds(block_of(lax.rem(y - k + ny, ny), core), span)]
        return pltpu.make_async_remote_copy(
            ref, ref, s_ac.at[2 * k + h], r_ac.at[2 * k + h], device_id=other_core, device_id_type=MESH
        )

    far_first = sorted(range(1, ny), key=lambda k: -min(k, ny - k))
    for h in range(2):
        lax.fori_loop(h * half // 2, (h + 1) * half // 2, average, 0, unroll=8)
        for k in far_first + [0]:
            to_core(k, h).start()
    for h in range(2):
        for k in far_first:
            place = at_y(k)[0]
            to_core(k, h).wait_recv()

            def pack(r, carry):
                a = share[core, place, 2 * r] + from_core[place, 2 * r]
                b = share[core, place, 2 * r + 1] + from_core[place, 2 * r + 1]
                send_y[k, r] = jnp.concatenate([a, b], axis=0).astype(BF16)
                return carry

            lax.fori_loop(h * half // 2, (h + 1) * half // 2, pack, 0, unroll=8)
            to_owner(k, h).start()

    def add_up(r, carry):
        a = share[core, y, 2 * r] + from_core[y, 2 * r]
        b = share[core, y, 2 * r + 1] + from_core[y, 2 * r + 1]
        value = jnp.concatenate([a, b], axis=0)
        for k in range(1, ny):
            value = value + from_y[k, r].astype(F32)
        total[pl.ds(pl.multiple_of(r * 2 * BINS, 2 * BINS), 2 * BINS), :] = value
        return carry

    for h in range(2):
        to_core(0, h).wait_recv()
        for k in far_first[::-1]:
            to_owner(k, h).wait_recv()
        lax.fori_loop(h * half // 2, (h + 1) * half // 2, add_up, 0, unroll=8)
        for g in range(BINS):
            block = total[pl.ds(h * half * BINS + g, half, stride=BINS), :].astype(BF16)
            aver[h * half:(h + 1) * half, pl.ds(pl.multiple_of(mine + g * BOX, BOX), BOX)] = block
        for k in far_first:
            along_y(k, h).start()
        across(0, h).start()

    mirror = (
        lax.broadcasted_iota(jnp.int32, (BOX, BOX), 0) + lax.broadcasted_iota(jnp.int32, (BOX, BOX), 1) == BOX - 1
    ).astype(F32).astype(BF16)

    def reverse(base, h):
        part = slice(h * half, (h + 1) * half)
        tiles = [aver[part, pl.ds(pl.multiple_of(base + g * BOX, BOX), BOX)] for g in range(BINS)]
        turned = dot(jnp.concatenate(tiles, axis=0), mirror).astype(BF16)
        part = slice(rows + h * half, rows + (h + 1) * half)
        for g in range(BINS):
            aver[part, pl.ds(pl.multiple_of(base + g * BOX, BOX), BOX)] = turned[g * half:(g + 1) * half]

    def project(base, lanes_at):
        return dot(aver[:, pl.ds(base, span)], weights[pl.ds(base, span), lanes_at])

    def add_block(base, first):
        for pair in range(nz // 2):
            at = slice(2 * pair * BOX, (2 * pair + 2) * BOX)
            block = project(base, at)
            planes[:, at] = block if first else planes[:, at] + block

    def back(k, which):
        return block_of(lax.rem(y - k + ny, ny), which)

    near_first = far_first[::-1]
    for h in range(2):
        reverse(back(0, core), h)
    add_block(back(0, core), True)
    for h in range(2):
        across(0, h).wait_recv()
        reverse(back(0, 1 - core), h)
    add_block(back(0, 1 - core), False)
    for k in near_first:
        along_y(k, 0).wait_recv()
        across(k, 0).start()
        reverse(back(k, core), 0)
    for k in near_first:
        along_y(k, 1).wait_recv()
        across(k, 1).start()
        reverse(back(k, core), 1)
        add_block(back(k, core), False)
        across(k, 0).wait_recv()
        reverse(back(k, 1 - core), 0)
    for k in near_first:
        across(k, 1).wait_recv()
        reverse(back(k, 1 - core), 1)
        if k != near_first[-1]:
            add_block(back(k, 1 - core), False)
    final = back(near_first[-1], 1 - core)

    def even_copy(k):
        return pltpu.make_async_remote_copy(
            give_e.at[k], take_e.at[k], s_e.at[k], r_e.at[k], device_id=at_z(k)[1], device_id_type=MESH
        )

    def odd_copy(k):
        device = ((nz - 1 - lax.rem(z + k, nz)) * nq + flip_q, slab)
        return pltpu.make_async_remote_copy(
            give_o.at[k], take_o.at[k], s_o.at[k], r_o.at[k], device_id=device, device_id_type=MESH
        )

    order = sorted(range(nz // 2), key=lambda pair: -min(2 * pair, nz - 2 * pair))
    for pair in order:
        at = slice(2 * pair * BOX, (2 * pair + 2) * BOX)
        block = planes[:, at] + project(final, at)
        for k in (2 * pair, 2 * pair + 1):
            at = (k - 2 * pair) * BOX
            give_e[k] = block[:rows, at:at + BOX].astype(BF16)
            give_o[k] = block[rows:, at:at + BOX].astype(BF16)
            odd_copy(k).start()
            if k:
                even_copy(k).start()

    for k in range(nz):
        odd_copy(k).wait()
        if k:
            even_copy(k).wait()
    for k in range(ny):
        for h in range(2):
            to_core(k, h).wait_send()
            across(k, h).wait_send()
            if k:
                to_owner(k, h).wait_send()
                along_y(k, h).wait_send()
    value = give_e[0].astype(F32)
    for k in range(1, nz):
        value = value + take_e[k].astype(F32)
    out[0] = value
    value = take_o[0].astype(F32)
    for k in range(1, nz):
        value = value + take_o[k].astype(F32)
    high, rest = split(value)
    middle = (value - high.astype(F32)).astype(BF16)
    lowest = (value - high.astype(F32) - middle.astype(F32)).astype(BF16)
    out[1] = dot(jnp.concatenate([high, middle, lowest], axis=1), jnp.concatenate([mirror] * 3, axis=0))


def body(nz, nq, ns, images, projections, regions, offsets, defocus, counts, tilt_angle):
    rows = BOX // ns
    pairs = rows // 2
    ny = nq // 2
    vmem = pl.BlockSpec(memory_space=pltpu.VMEM)
    dma = pltpu.SemaphoreType.DMA
    scratch = [
        pltpu.VMEM((PART, BOX, BOX), BF16),
        pltpu.VMEM((BINS, rows, BOX), BF16),
        pltpu.VMEM((3 * BOX, BOX), BF16),
        pltpu.VMEM((4 * PART * 8, BOX), F32),
        pltpu.VMEM((PART * rows, BOX), F32),
        pltpu.VMEM((nz, rows, PART, BOX), BF16),
        pltpu.VMEM((nq, rows // 4, 2 * BINS, 2 * BOX), BF16),
        pltpu.VMEM((nq, 24, BOX), F32),
        pltpu.VMEM((nz, 8, BOX), jnp.int32),
        pltpu.VMEM((ns, 2 * BINS, nz * PART), F32),
        pltpu.VMEM((nz, 8, BOX), F32),
        pltpu.VMEM((2, ny, rows, BINS, BOX), F32),
        pltpu.VMEM((ny, rows, BINS, BOX), F32),
        pltpu.VMEM((ny, pairs, 2 * BINS, BOX), BF16),
        pltpu.VMEM((ny, pairs, 2 * BINS, BOX), BF16),
        pltpu.VMEM((rows * BINS, BOX), F32),
        pltpu.VMEM((2 * rows, nq * BINS * BOX), BF16),
        pltpu.VMEM((nq * BINS * BOX, nz * BOX), BF16),
        pltpu.VMEM((2 * rows, nz * BOX), F32),
        pltpu.VMEM((nz, rows, BOX), BF16),
        pltpu.VMEM((nz, rows, BOX), BF16),
        pltpu.VMEM((nz, rows, BOX), BF16),
        pltpu.VMEM((nz, rows, BOX), BF16),
    ]
    scratch.append(dma((3,)))
    steps = PIECES * (nz - 1) // 2
    for count in (nq, nq, nz, steps, steps, ns, nz, 2 * ny, 2 * ny, 2 * ny, 2 * ny, nz, nz):
        scratch += [dma((count,)), dma((count,))]
    return pl.pallas_call(
        functools.partial(kernel, nz, nq, ns),
        out_shape=pltpu.VMEM((2, rows, BOX), F32),
        in_specs=[pl.BlockSpec(memory_space=pltpu.SMEM)] * 5 + [pl.BlockSpec(memory_space=pl.ANY)] * 3,
        out_specs=vmem,
        scratch_shapes=scratch,
        compiler_params=pltpu.CompilerParams(
            collective_id=0, has_side_effects=True, vmem_limit_bytes=60 * 1024 * 1024
        ),
    )(regions.T, offsets, defocus, counts, tilt_angle, images, projections, jnp.asarray(cosine_table()))


def solution(mesh):
    nq = PLANE_GROUP
    nz = mesh.shape["bins"] // nq
    ns = mesh.shape["slab"]
    in_specs = (
        P("bins", None, None),
        P("bins", None, None),
        P("bins", None),
        P(None, "bins"),
        P("bins"),
        P("bins"),
        P("bins"),
    )
    return jax.shard_map(
        functools.partial(body, nz, nq, ns),
        mesh=mesh,
        in_specs=in_specs,
        out_specs=P("bins", "slab", None),
        check_vma=False,
    )
```

```python
import functools

import jax
import jax.numpy as jnp
import ml_dtypes
import numpy as np
from jax import lax
from jax.experimental import pallas as pl
from jax.experimental.pallas import tpu as pltpu
from jax.sharding import PartitionSpec as P

AMP_COS = 0.1
AMP_SIN = 0.99498743710662
CHI_SCALE = 100.0
ENVELOPE = 8.0
BOX = 128
PART = 16
BINS = 8
PLANE_GROUP = 8
PIECES = 4
MESH = pl.DeviceIdType.MESH
F32 = jnp.float32
BF16 = jnp.bfloat16


def cosine_table():
    i = np.arange(BOX)
    cosine = np.cos(2.0 * np.pi / BOX * (i[:, None] * i[None, :] % BOX))
    high = cosine.astype(ml_dtypes.bfloat16)
    low = (cosine - high.astype(np.float64)).astype(ml_dtypes.bfloat16)
    return np.concatenate([high, high, low], axis=0)


def split(value):
    high = value.astype(BF16)
    return high, (value - high.astype(F32)).astype(BF16)


def dot(a, b):
    return jnp.dot(a, b, preferred_element_type=F32)


def dot_nt(a, b):
    return lax.dot_general(a, b, (((1,), (1,)), ((), ())), preferred_element_type=F32)


def kernel(
    nz, nq, ns,
    regions, offs, defocus, counts, tilt, images_hbm, proj_hbm, table_hbm,
    out,
    imgs, proj, table, taps, staged, frames, refs, meta_p, meta_z, partial, stats, share, from_core, send_y, from_y, total,
    aver, weights, planes, give_e, give_o, take_e, take_o,
    s_in, s_mp, r_mp, s_pr, r_pr, s_mz, r_mz, s_rt, r_rt, s_lf, r_lf, s_x, r_x, s_st, r_st,
    s_rc, r_rc, s_ry, r_ry, s_ac, r_ac, s_ay, r_ay, s_e, r_e, s_o, r_o,
):
    rows = BOX // ns
    pairs = rows // 2
    ny = nq // 2
    quarter = rows // PIECES
    depth = 2 * nz * nq
    me = lax.axis_index("bins")
    slab = lax.axis_index("slab")
    z = me // nq
    q = lax.rem(me, nq)
    flip_q = nq - 1 - q
    y = q // 2
    core = lax.rem(q, 2)
    other_core = (z * nq + 2 * y + 1 - core, slab)
    centre = (BOX - 1) / 2.0

    def at_q(k):
        other = lax.rem(q + k, nq)
        return other, (z * nq + other, slab)

    def at_z(k):
        other = lax.rem(z + k, nz)
        return other, (other * nq + q, slab)

    def at_y(k):
        other = lax.rem(y + k, ny)
        return other, (z * nq + 2 * other + core, slab)

    first_row = pl.multiple_of(slab * rows, rows)
    loads = [
        pltpu.make_async_copy(src, dst, s_in.at[i])
        for i, (src, dst) in enumerate(
            (
                (table_hbm, table),
                (images_hbm, imgs),
                (proj_hbm.at[:, pl.ds(first_row, rows)], proj),
            )
        )
    ]
    for load in loads:
        load.start()

    barrier = pltpu.get_barrier_semaphore()
    partners = [at_q(k)[1] for k in range(1, nq)] + [at_z(k)[1] for k in range(1, nz)]
    partners += [(lax.rem(z + k, nz) * nq + flip_q, slab) for k in range(1, nz)]
    partners += [(me, lax.rem(slab + k, ns)) for k in range(1, ns)]
    for device in partners:
        pl.semaphore_signal(barrier, inc=1, device_id=device, device_id_type=MESH)

    lane = lax.broadcasted_iota(jnp.int32, (8, BOX), 1)
    line = lax.broadcasted_iota(jnp.int32, (8, BOX), 0)
    angle = jnp.zeros((8, BOX), F32)
    count = jnp.zeros((8, BOX), jnp.int32)
    for g in range(BINS):
        angle = jnp.where(line == g, tilt[g], angle)
        count = jnp.where(line == g, counts[g], count)
    meta_p[q, 0:8, :] = jnp.log(1.0 + count.astype(F32))
    meta_p[q, 8:16, :] = jnp.cos(angle)
    meta_p[q, 16:24, :] = jnp.sin(angle)
    named = jnp.zeros((8, BOX), jnp.int32)
    for p in range(PART):
        for t in range(2):
            named = jnp.where((lane == z * PART + p) & (line == t), regions[t, p], named)
    meta_z[z] = named

    index = lax.broadcasted_iota(jnp.int32, (PART, BOX), 1)
    which = lax.broadcasted_iota(jnp.int32, (PART, BOX), 0)
    blur = jnp.zeros((PART, BOX), F32)
    for p in range(PART):
        blur = jnp.where(which == p, defocus[p], blur)
    freq = jnp.where(index < BOX // 2, index, index - BOX).astype(F32) / BOX
    square = freq * freq
    phase = CHI_SCALE * blur * square
    fade = jnp.exp(-ENVELOPE * square)
    sine, cosine = jnp.sin(phase), jnp.cos(phase)
    gains = jnp.concatenate(
        [
            -fade * (AMP_SIN * sine + AMP_COS * cosine),
            -fade * (AMP_SIN * cosine - AMP_COS * sine),
            fade * cosine,
            fade * sine,
        ],
        axis=0,
    )
    gh, gl = split(gains * (1.0 / BOX))
    loads[0].wait()
    found = dot(jnp.concatenate([gh, gl, gh], axis=1), table[...])
    for k in range(8):
        taps[pl.ds(k, 4 * PART, stride=8), :] = pltpu.roll(found, k, 1) if k else found

    loads[2].wait()
    for g in range(BINS):
        staged[g * rows:(g + 1) * rows, :] = proj[g].astype(F32)
    for r in range(rows // 4):
        lines = [staged[pl.ds(4 * r + k, BINS, stride=rows), :] for k in range(4)]
        upper, lower = jnp.concatenate(lines[:2], axis=1), jnp.concatenate(lines[2:], axis=1)
        refs[q, r] = jnp.concatenate([upper, lower], axis=0).astype(BF16)

    def circulant(index, count, shift):
        eight = taps[pl.ds(pl.multiple_of(index * 8, 8), 8), :]
        return [pltpu.roll(eight, lax.rem(shift + 8 * k, BOX), 1) for k in range(count // 8)]

    def filter_one(p):
        down = lax.rem(slab * rows - offs[0, p] + 2 * BOX, BOX)
        along = lax.rem(offs[1, p] + BOX, BOX)
        left = jnp.concatenate(circulant(p, rows, down) + circulant(PART + p, rows, down), axis=0)
        t = dot(jnp.concatenate(split(left), axis=0), imgs[p])
        t = t[:2 * rows] + t[2 * rows:]
        t = jnp.concatenate([t[:rows], t[rows:]], axis=1)
        right = circulant(2 * PART + p, BOX, along) + circulant(3 * PART + p, BOX, along)
        right = jnp.concatenate(right, axis=0)
        out = dot(jnp.concatenate(split(t), axis=0), jnp.concatenate(split(right), axis=1))
        out = out[:, :BOX] + out[:, BOX:]
        staged[pl.ds(pl.multiple_of(p * rows, rows), rows), :] = out[:rows] + out[rows:]

    def filter_some(step, carry):
        for k in range(8):
            filter_one(step * 8 + k)
        return carry

    loads[1].wait()
    lax.fori_loop(0, PART // 8, filter_some, 0)
    for r in range(rows):
        frames[z, r] = staged[pl.ds(r, PART, stride=rows), :].astype(BF16)

    pl.semaphore_wait(barrier, len(partners))

    def to_q(buf, send, recv, k):
        device = at_q(k)[1]
        return pltpu.make_async_remote_copy(buf.at[q], buf.at[q], send.at[k], recv.at[k], device_id=device, device_id_type=MESH)

    def to_z(buf, send, recv, k):
        device = at_z(k)[1]
        return pltpu.make_async_remote_copy(buf.at[z], buf.at[z], send.at[k], recv.at[k], device_id=device, device_id_type=MESH)

    def ring(step, sign, send, recv):
        source = lax.rem(z + (nz - sign * (step // PIECES)), nz)
        piece = step % PIECES if sign > 0 else PIECES - 1 - step % PIECES
        ref = frames.at[source, pl.ds(piece * quarter, quarter)]
        device = (lax.rem(z + nz + sign, nz) * nq + q, slab)
        return pltpu.make_async_remote_copy(ref, ref, send.at[step], recv.at[step], device_id=device, device_id_type=MESH)

    def right(step):
        return ring(step, 1, s_rt, r_rt)

    def left(step):
        return ring(step, -1, s_lf, r_lf)

    steps = PIECES * (nz - 1) // 2
    for step in range(PIECES):
        right(step).start()
        left(step).start()
    for k in range(1, nq):
        to_q(meta_p, s_mp, r_mp, k).start()
    for k in range(1, nz):
        to_z(meta_z, s_mz, r_mz, k).start()
    for k in range(1, nq):
        to_q(refs, s_pr, r_pr, k).start()
    for k in range(1, nq):
        to_q(meta_p, s_mp, r_mp, k).wait_recv()

    column = lax.broadcasted_iota(jnp.int32, (1, BOX), 1).astype(F32) - centre
    height = lax.broadcasted_iota(jnp.int32, (BOX, BOX), 0).astype(F32)

    def weigh(unit):
        j = unit // 2

        def one(g, carry):
            cosr = meta_p[j, pl.ds(8 + g, 1), :]
            sinr = meta_p[j, pl.ds(16 + g, 1), :]
            base = pl.multiple_of((j * BINS + g) * BOX, BOX)
            for k in range(nz):
                plane = 2 * (lax.rem(z + k, nz) * nq + q)
                away = plane.astype(F32) - (depth - 1) / 2.0
                landing = column * cosr + away * sinr + centre
                w = jnp.maximum(0.0, 1.0 - jnp.abs(landing - height))
                weights[pl.ds(base, BOX), k * BOX:(k + 1) * BOX] = w.astype(BF16)
            return carry

        first = unit % 2 * (BINS // 2)
        lax.fori_loop(first, first + BINS // 2, one, 0)

    units = 2 * nq
    for step in range(steps):
        right(step).wait_recv()
        if step + PIECES < steps:
            right(step + PIECES).start()
        left(step).wait_recv()
        if step + PIECES < steps:
            left(step + PIECES).start()

    for k in range(1, nq):
        to_q(refs, s_pr, r_pr, k).wait_recv()
    for k in range(1, nz):
        to_z(meta_z, s_mz, r_mz, k).wait_recv()

    lanes = nz * PART

    def frame(r):
        return frames[:, r].reshape(lanes, BOX)

    def frame_pair(r):
        return jnp.concatenate([frame(2 * r), frame(2 * r + 1)], axis=1)

    def score(r, found):
        a = refs[:, r].reshape(nq * 2 * BINS, 2 * BOX)
        return found + dot_nt(a, jnp.concatenate([frame_pair(2 * r), frame_pair(2 * r + 1)], axis=0))

    found = jnp.zeros((nq * 2 * BINS, 2 * lanes), F32)
    found = lax.fori_loop(0, rows // 4, score, found, unroll=4).reshape(nq, 2, BINS, 2 * lanes)
    scores = found[:, 0, :, :lanes] + found[:, 1, :, lanes:]

    named = meta_z[0]
    for k in range(1, nz):
        named = named + meta_z[k]
    prior = meta_p[:, 0:8, :lanes]
    held, priors = [], []
    for t in range(2):
        place = named[t:t + 1, :lanes] - z * nq
        chosen = jnp.zeros((BINS, lanes), F32)
        chance = jnp.zeros((BINS, lanes), F32)
        for j in range(nq):
            chosen = jnp.where(place == j, scores[j], chosen)
            chance = jnp.where(place == j, prior[j], chance)
        partial[slab, t * BINS:(t + 1) * BINS, :] = chosen
        priors.append(chance)
        held.append((place >= 0) & (place < nq))

    def to_x(k):
        device = (me, lax.rem(slab + k, ns))
        return pltpu.make_async_remote_copy(
            partial.at[slab], partial.at[slab], s_x.at[k], r_x.at[k], device_id=device, device_id_type=MESH
        )

    for k in range(1, ns):
        to_x(k).start()
    for unit in range(units // 3):
        weigh(unit)
    for k in range(1, ns):
        to_x(k).wait_recv()
    scores = partial[0]
    for k in range(1, ns):
        scores = scores + partial[k]
    low = jnp.float32(-3.0e38)
    logits = [scores[t * BINS:(t + 1) * BINS] / BOX + priors[t] for t in range(2)]
    tops = [jnp.where(held[t], jnp.max(logits[t], axis=0, keepdims=True), low) for t in range(2)]
    top = jnp.maximum(tops[0], tops[1])
    summed = jnp.zeros((1, lanes), F32)
    for t in range(2):
        grown = jnp.exp(jnp.where(held[t], logits[t] - top, low))
        summed = summed + jnp.sum(grown, axis=0, keepdims=True)
    stats[z, 0:1, :lanes] = top
    stats[z, 1:2, :lanes] = summed
    for k in range(1, nz):
        to_z(stats, s_st, r_st, k).start()
    for unit in range(units // 3, units):
        weigh(unit)
    for step in range(steps):
        right(step).wait_send()
        left(step).wait_send()
    for k in range(1, nq):
        to_q(meta_p, s_mp, r_mp, k).wait_send()
        to_q(refs, s_pr, r_pr, k).wait_send()
    for k in range(1, ns):
        to_x(k).wait_send()
    for k in range(1, nz):
        to_z(meta_z, s_mz, r_mz, k).wait_send()
        to_z(stats, s_st, r_st, k).wait_recv()
    best = stats[0, 0:1, :lanes]
    for k in range(1, nz):
        best = jnp.maximum(best, stats[k, 0:1, :lanes])
    whole = jnp.zeros((1, lanes), F32)
    for k in range(nz):
        whole = whole + stats[k, 1:2, :lanes] * jnp.exp(stats[k, 0:1, :lanes] - best)
    norm = best + jnp.log(whole)
    chances = [jnp.exp(jnp.where(held[t], logits[t] - norm, low)) for t in range(2)]
    posterior = []
    for j in range(nq):
        value = jnp.zeros((BINS, lanes), F32)
        for t in range(2):
            place = named[t:t + 1, :lanes] - z * nq
            value = jnp.where(place == j, chances[t], value)
        posterior.append(value)
    posterior = jnp.concatenate(posterior, axis=0).astype(BF16)

    def average(r, carry):
        a = dot(posterior, frame_pair(r)).reshape(ny, 2, BINS, 2 * BOX)
        for which in range(2):
            share[which, :, 2 * r] = a[:, which, :, :BOX]
            share[which, :, 2 * r + 1] = a[:, which, :, BOX:]
        return carry

    half = rows // 2

    def to_core(k, h):
        place = at_y(k)[0]
        part = pl.ds(h * half, half)
        return pltpu.make_async_remote_copy(
            share.at[1 - core, place, part], from_core.at[place, part], s_rc.at[2 * k + h], r_rc.at[2 * k + h],
            device_id=other_core, device_id_type=MESH,
        )

    def to_owner(k, h):
        part = pl.ds(h * half // 2, half // 2)
        return pltpu.make_async_remote_copy(
            send_y.at[k, part], from_y.at[k, part], s_ry.at[2 * k + h], r_ry.at[2 * k + h],
            device_id=at_y(k)[1], device_id_type=MESH,
        )

    span = BINS * BOX
    mine = pl.multiple_of(q * span, span)

    def block_of(place, which):
        return pl.multiple_of((2 * place + which) * span, span)

    def along_y(k, h):
        ref = aver.at[pl.ds(h * half, half), pl.ds(mine, span)]
        return pltpu.make_async_remote_copy(
            ref, ref, s_ay.at[2 * k + h], r_ay.at[2 * k + h], device_id=at_y(k)[1], device_id_type=MESH
        )

    def across(k, h):
        ref = aver.at[pl.ds(h * half, half), pl.ds(block_of(lax.rem(y - k + ny, ny), core), span)]
        return pltpu.make_async_remote_copy(
            ref, ref, s_ac.at[2 * k + h], r_ac.at[2 * k + h], device_id=other_core, device_id_type=MESH
        )

    far_first = sorted(range(1, ny), key=lambda k: -min(k, ny - k))
    for h in range(2):
        lax.fori_loop(h * half // 2, (h + 1) * half // 2, average, 0, unroll=8)
        for k in far_first + [0]:
            to_core(k, h).start()
    for h in range(2):
        for k in far_first:
            place = at_y(k)[0]
            to_core(k, h).wait_recv()

            def pack(r, carry):
                a = share[core, place, 2 * r] + from_core[place, 2 * r]
                b = share[core, place, 2 * r + 1] + from_core[place, 2 * r + 1]
                send_y[k, r] = jnp.concatenate([a, b], axis=0).astype(BF16)
                return carry

            lax.fori_loop(h * half // 2, (h + 1) * half // 2, pack, 0, unroll=8)
            to_owner(k, h).start()

    def add_up(r, carry):
        a = share[core, y, 2 * r] + from_core[y, 2 * r]
        b = share[core, y, 2 * r + 1] + from_core[y, 2 * r + 1]
        value = jnp.concatenate([a, b], axis=0)
        for k in range(1, ny):
            value = value + from_y[k, r].astype(F32)
        total[pl.ds(pl.multiple_of(r * 2 * BINS, 2 * BINS), 2 * BINS), :] = value
        return carry

    for h in range(2):
        to_core(0, h).wait_recv()
        for k in far_first[::-1]:
            to_owner(k, h).wait_recv()
        lax.fori_loop(h * half // 2, (h + 1) * half // 2, add_up, 0, unroll=8)
        for g in range(BINS):
            block = total[pl.ds(h * half * BINS + g, half, stride=BINS), :].astype(BF16)
            aver[h * half:(h + 1) * half, pl.ds(pl.multiple_of(mine + g * BOX, BOX), BOX)] = block
        for k in far_first:
            along_y(k, h).start()
        across(0, h).start()

    mirror = (
        lax.broadcasted_iota(jnp.int32, (BOX, BOX), 0) + lax.broadcasted_iota(jnp.int32, (BOX, BOX), 1) == BOX - 1
    ).astype(F32).astype(BF16)

    def reverse(base, h):
        part = slice(h * half, (h + 1) * half)
        tiles = [aver[part, pl.ds(pl.multiple_of(base + g * BOX, BOX), BOX)] for g in range(BINS)]
        turned = dot(jnp.concatenate(tiles, axis=0), mirror).astype(BF16)
        part = slice(rows + h * half, rows + (h + 1) * half)
        for g in range(BINS):
            aver[part, pl.ds(pl.multiple_of(base + g * BOX, BOX), BOX)] = turned[g * half:(g + 1) * half]

    def project(base, lanes_at):
        return dot(aver[:, pl.ds(base, span)], weights[pl.ds(base, span), lanes_at])

    def add_block(base, first):
        for pair in range(nz // 2):
            at = slice(2 * pair * BOX, (2 * pair + 2) * BOX)
            block = project(base, at)
            planes[:, at] = block if first else planes[:, at] + block

    def back(k, which):
        return block_of(lax.rem(y - k + ny, ny), which)

    near_first = far_first[::-1]
    for h in range(2):
        reverse(back(0, core), h)
    add_block(back(0, core), True)
    for h in range(2):
        across(0, h).wait_recv()
        reverse(back(0, 1 - core), h)
    add_block(back(0, 1 - core), False)
    for k in near_first:
        along_y(k, 0).wait_recv()
        across(k, 0).start()
        reverse(back(k, core), 0)
    for k in near_first:
        along_y(k, 1).wait_recv()
        across(k, 1).start()
        reverse(back(k, core), 1)
        add_block(back(k, core), False)
        across(k, 0).wait_recv()
        reverse(back(k, 1 - core), 0)
    for k in near_first:
        across(k, 1).wait_recv()
        reverse(back(k, 1 - core), 1)
        if k != near_first[-1]:
            add_block(back(k, 1 - core), False)
    final = back(near_first[-1], 1 - core)

    def even_copy(k):
        return pltpu.make_async_remote_copy(
            give_e.at[k], take_e.at[k], s_e.at[k], r_e.at[k], device_id=at_z(k)[1], device_id_type=MESH
        )

    def odd_copy(k):
        device = ((nz - 1 - lax.rem(z + k, nz)) * nq + flip_q, slab)
        return pltpu.make_async_remote_copy(
            give_o.at[k], take_o.at[k], s_o.at[k], r_o.at[k], device_id=device, device_id_type=MESH
        )

    order = sorted(range(nz // 2), key=lambda pair: -min(2 * pair, nz - 2 * pair))
    for pair in order:
        at = slice(2 * pair * BOX, (2 * pair + 2) * BOX)
        block = planes[:, at] + project(final, at)
        for k in (2 * pair, 2 * pair + 1):
            at = (k - 2 * pair) * BOX
            give_e[k] = block[:rows, at:at + BOX].astype(BF16)
            give_o[k] = block[rows:, at:at + BOX].astype(BF16)
            odd_copy(k).start()
            if k:
                even_copy(k).start()

    for k in range(1, nz):
        to_z(stats, s_st, r_st, k).wait_send()
    for k in range(ny):
        for h in range(2):
            to_core(k, h).wait_send()
            across(k, h).wait_send()
            if k:
                to_owner(k, h).wait_send()
                along_y(k, h).wait_send()
    for k in range(nz):
        odd_copy(k).wait_send()
        if k:
            even_copy(k).wait_send()
    value = give_e[0].astype(F32)
    for k in sorted(range(1, nz), key=lambda k: min(k, nz - k)):
        even_copy(k).wait_recv()
        value = value + take_e[k].astype(F32)
    out[0] = value
    for k in range(nz):
        odd_copy(k).wait_recv()
    out[1] = dot(
        jnp.concatenate([take_o[k] for k in range(nz)], axis=1), jnp.concatenate([mirror] * nz, axis=0)
    )


def body(nz, nq, ns, images, projections, regions, offsets, defocus, counts, tilt_angle):
    rows = BOX // ns
    pairs = rows // 2
    ny = nq // 2
    vmem = pl.BlockSpec(memory_space=pltpu.VMEM)
    dma = pltpu.SemaphoreType.DMA
    scratch = [
        pltpu.VMEM((PART, BOX, BOX), BF16),
        pltpu.VMEM((BINS, rows, BOX), BF16),
        pltpu.VMEM((3 * BOX, BOX), BF16),
        pltpu.VMEM((4 * PART * 8, BOX), F32),
        pltpu.VMEM((PART * rows, BOX), F32),
        pltpu.VMEM((nz, rows, PART, BOX), BF16),
        pltpu.VMEM((nq, rows // 4, 2 * BINS, 2 * BOX), BF16),
        pltpu.VMEM((nq, 24, BOX), F32),
        pltpu.VMEM((nz, 8, BOX), jnp.int32),
        pltpu.VMEM((ns, 2 * BINS, nz * PART), F32),
        pltpu.VMEM((nz, 8, BOX), F32),
        pltpu.VMEM((2, ny, rows, BINS, BOX), F32),
        pltpu.VMEM((ny, rows, BINS, BOX), F32),
        pltpu.VMEM((ny, pairs, 2 * BINS, BOX), BF16),
        pltpu.VMEM((ny, pairs, 2 * BINS, BOX), BF16),
        pltpu.VMEM((rows * BINS, BOX), F32),
        pltpu.VMEM((2 * rows, nq * BINS * BOX), BF16),
        pltpu.VMEM((nq * BINS * BOX, nz * BOX), BF16),
        pltpu.VMEM((2 * rows, nz * BOX), F32),
        pltpu.VMEM((nz, rows, BOX), BF16),
        pltpu.VMEM((nz, rows, BOX), BF16),
        pltpu.VMEM((nz, rows, BOX), BF16),
        pltpu.VMEM((nz, rows, BOX), BF16),
    ]
    scratch.append(dma((3,)))
    steps = PIECES * (nz - 1) // 2
    for count in (nq, nq, nz, steps, steps, ns, nz, 2 * ny, 2 * ny, 2 * ny, 2 * ny, nz, nz):
        scratch += [dma((count,)), dma((count,))]
    return pl.pallas_call(
        functools.partial(kernel, nz, nq, ns),
        out_shape=pltpu.VMEM((2, rows, BOX), F32),
        in_specs=[pl.BlockSpec(memory_space=pltpu.SMEM)] * 5 + [pl.BlockSpec(memory_space=pl.ANY)] * 3,
        out_specs=vmem,
        scratch_shapes=scratch,
        compiler_params=pltpu.CompilerParams(
            collective_id=0, has_side_effects=True, vmem_limit_bytes=60 * 1024 * 1024
        ),
    )(regions.T, offsets, defocus, counts, tilt_angle, images, projections, jnp.asarray(cosine_table()))


def solution(mesh):
    nq = PLANE_GROUP
    nz = mesh.shape["bins"] // nq
    ns = mesh.shape["slab"]
    in_specs = (
        P("bins", None, None),
        P("bins", None, None),
        P("bins", None),
        P(None, "bins"),
        P("bins"),
        P("bins"),
        P("bins"),
    )
    return jax.shard_map(
        functools.partial(body, nz, nq, ns),
        mesh=mesh,
        in_specs=in_specs,
        out_specs=P("bins", "slab", None),
        check_vma=False,
    )
```

```python
import functools

import jax
import jax.numpy as jnp
import ml_dtypes
import numpy as np
from jax import lax
from jax.experimental import pallas as pl
from jax.experimental.pallas import tpu as pltpu
from jax.sharding import PartitionSpec as P

AMP_COS = 0.1
AMP_SIN = 0.99498743710662
CHI_SCALE = 100.0
ENVELOPE = 8.0
BOX = 128
PART = 16
BINS = 8
PLANE_GROUP = 8
PIECES = 4
MESH = pl.DeviceIdType.MESH
F32 = jnp.float32
BF16 = jnp.bfloat16


def cosine_table():
    i = np.arange(BOX)
    cosine = np.cos(2.0 * np.pi / BOX * (i[:, None] * i[None, :] % BOX))
    high = cosine.astype(ml_dtypes.bfloat16)
    low = (cosine - high.astype(np.float64)).astype(ml_dtypes.bfloat16)
    return np.concatenate([high, high, low], axis=0)


def split(value):
    high = value.astype(BF16)
    return high, (value - high.astype(F32)).astype(BF16)


def dot(a, b):
    return jnp.dot(a, b, preferred_element_type=F32)


def dot_nt(a, b):
    return lax.dot_general(a, b, (((1,), (1,)), ((), ())), preferred_element_type=F32)


def kernel(
    nz, nq, ns,
    regions, offs, defocus, counts, tilt, images_hbm, proj_hbm, table_hbm,
    out,
    imgs, proj, table, taps, staged, frames, refs, meta_p, meta_z, partial, stats, share, from_core, send_y, from_y, total,
    aver, weights, planes, give_e, give_o, take_e, take_o,
    s_in, s_mp, r_mp, s_pr, r_pr, s_mz, r_mz, s_rt, r_rt, s_lf, r_lf, s_x, r_x, s_st, r_st,
    s_rc, r_rc, s_ry, r_ry, s_ac, r_ac, s_ay, r_ay, s_e, r_e, s_o, r_o,
):
    rows = BOX // ns
    pairs = rows // 2
    ny = nq // 2
    quarter = rows // PIECES
    depth = 2 * nz * nq
    me = lax.axis_index("bins")
    slab = lax.axis_index("slab")
    z = me // nq
    q = lax.rem(me, nq)
    y = q // 2
    core = lax.rem(q, 2)
    mate = q + 1 - 2 * core
    flip_q = nq - 1 - mate
    other_core = (z * nq + 2 * y + 1 - core, slab)
    centre = (BOX - 1) / 2.0

    def at_q(k):
        other = lax.rem(q + k, nq)
        return other, (z * nq + other, slab)

    def at_z(k):
        other = lax.rem(z + k, nz)
        return other, (other * nq + q, slab)

    def at_y(k):
        other = lax.rem(y + k, ny)
        return other, (z * nq + 2 * other + core, slab)

    first_row = pl.multiple_of(slab * rows, rows)
    loads = [
        pltpu.make_async_copy(src, dst, s_in.at[i])
        for i, (src, dst) in enumerate(
            (
                (table_hbm, table),
                (images_hbm, imgs),
                (proj_hbm.at[:, pl.ds(first_row, rows)], proj),
            )
        )
    ]
    for load in loads:
        load.start()

    barrier = pltpu.get_barrier_semaphore()
    partners = [at_q(k)[1] for k in range(1, nq)] + [at_z(k)[1] for k in range(1, nz)]
    partners += [(lax.rem(z + k, nz) * nq + other, slab) for k in range(1, nz) for other in (mate, flip_q)]
    partners += [(me, lax.rem(slab + k, ns)) for k in range(1, ns)]
    for device in partners:
        pl.semaphore_signal(barrier, inc=1, device_id=device, device_id_type=MESH)

    index = lax.broadcasted_iota(jnp.int32, (PART, BOX), 1)
    which = lax.broadcasted_iota(jnp.int32, (PART, BOX), 0)
    blur = jnp.zeros((PART, BOX), F32)
    for p in range(PART):
        blur = jnp.where(which == p, defocus[p], blur)
    freq = jnp.where(index < BOX // 2, index, index - BOX).astype(F32) / BOX
    square = freq * freq
    phase = CHI_SCALE * blur * square
    fade = jnp.exp(-ENVELOPE * square)
    sine, cosine = jnp.sin(phase), jnp.cos(phase)
    gains = jnp.concatenate(
        [
            -fade * (AMP_SIN * sine + AMP_COS * cosine),
            -fade * (AMP_SIN * cosine - AMP_COS * sine),
            fade * cosine,
            fade * sine,
        ],
        axis=0,
    )
    gh, gl = split(gains * (1.0 / BOX))
    loads[0].wait()
    found = dot(jnp.concatenate([gh, gl, gh], axis=1), table[...])
    for k in range(8):
        taps[pl.ds(k, 4 * PART, stride=8), :] = pltpu.roll(found, k, 1) if k else found

    def circulant(index, count, shift):
        eight = taps[pl.ds(pl.multiple_of(index * 8, 8), 8), :]
        return [pltpu.roll(eight, lax.rem(shift + 8 * k, BOX), 1) for k in range(count // 8)]

    def filter_one(p):
        down = lax.rem(slab * rows - offs[0, p] + 2 * BOX, BOX)
        along = lax.rem(offs[1, p] + BOX, BOX)
        left = jnp.concatenate(circulant(p, rows, down) + circulant(PART + p, rows, down), axis=0)
        t = dot(jnp.concatenate(split(left), axis=0), imgs[p])
        t = t[:2 * rows] + t[2 * rows:]
        t = jnp.concatenate([t[:rows], t[rows:]], axis=1)
        right = circulant(2 * PART + p, BOX, along) + circulant(3 * PART + p, BOX, along)
        right = jnp.concatenate(right, axis=0)
        out = dot(jnp.concatenate(split(t), axis=0), jnp.concatenate(split(right), axis=1))
        out = out[:, :BOX] + out[:, BOX:]
        staged[pl.ds(pl.multiple_of(p * rows, rows), rows), :] = out[:rows] + out[rows:]

    def filter_some(step, carry):
        for k in range(16):
            filter_one(step * 16 + k)
        return carry

    loads[1].wait()
    lax.fori_loop(0, PART // 16, filter_some, 0)
    for r in range(rows):
        frames[z, r] = staged[pl.ds(r, PART, stride=rows), :].astype(BF16)

    pl.semaphore_wait(barrier, len(partners))

    def to_q(buf, send, recv, k):
        device = at_q(k)[1]
        return pltpu.make_async_remote_copy(buf.at[q], buf.at[q], send.at[k], recv.at[k], device_id=device, device_id_type=MESH)

    def to_z(buf, send, recv, k):
        device = at_z(k)[1]
        return pltpu.make_async_remote_copy(buf.at[z], buf.at[z], send.at[k], recv.at[k], device_id=device, device_id_type=MESH)

    def ring(step, sign, send, recv):
        source = lax.rem(z + (nz - sign * (step // PIECES)), nz)
        piece = step % PIECES if sign > 0 else PIECES - 1 - step % PIECES
        ref = frames.at[source, pl.ds(piece * quarter, quarter)]
        device = (lax.rem(z + nz + sign, nz) * nq + q, slab)
        return pltpu.make_async_remote_copy(ref, ref, send.at[step], recv.at[step], device_id=device, device_id_type=MESH)

    def right(step):
        return ring(step, 1, s_rt, r_rt)

    def left(step):
        return ring(step, -1, s_lf, r_lf)

    steps = PIECES * (nz - 1) // 2
    for step in range(PIECES):
        right(step).start()
        left(step).start()

    lane = lax.broadcasted_iota(jnp.int32, (8, BOX), 1)
    line = lax.broadcasted_iota(jnp.int32, (8, BOX), 0)
    angle = jnp.zeros((8, BOX), F32)
    count = jnp.zeros((8, BOX), jnp.int32)
    for g in range(BINS):
        angle = jnp.where(line == g, tilt[g], angle)
        count = jnp.where(line == g, counts[g], count)
    meta_p[q, 0:8, :] = jnp.log(1.0 + count.astype(F32))
    meta_p[q, 8:16, :] = jnp.cos(angle)
    meta_p[q, 16:24, :] = jnp.sin(angle)
    named = jnp.zeros((8, BOX), jnp.int32)
    for p in range(PART):
        for t in range(2):
            named = jnp.where((lane == z * PART + p) & (line == t), regions[t, p], named)
    meta_z[z] = named

    for k in range(1, nq):
        to_q(meta_p, s_mp, r_mp, k).start()
    for k in range(1, nz):
        to_z(meta_z, s_mz, r_mz, k).start()
    loads[2].wait()
    for g in range(BINS):
        staged[g * rows:(g + 1) * rows, :] = proj[g].astype(F32)
    for r in range(rows // 4):
        lines = [staged[pl.ds(4 * r + k, BINS, stride=rows), :] for k in range(4)]
        upper, lower = jnp.concatenate(lines[:2], axis=1), jnp.concatenate(lines[2:], axis=1)
        refs[q, r] = jnp.concatenate([upper, lower], axis=0).astype(BF16)
    for k in range(1, nq):
        to_q(refs, s_pr, r_pr, k).start()
    for k in range(1, nq):
        to_q(meta_p, s_mp, r_mp, k).wait_recv()

    column = lax.broadcasted_iota(jnp.int32, (1, BOX), 1).astype(F32) - centre
    height = lax.broadcasted_iota(jnp.int32, (BOX, BOX), 0).astype(F32)

    def weigh(unit):
        j = unit // 2

        def one(g, carry):
            cosr = meta_p[j, pl.ds(8 + g, 1), :]
            sinr = meta_p[j, pl.ds(16 + g, 1), :]
            base = pl.multiple_of((j * BINS + g) * BOX, BOX)
            for k in range(nz):
                plane = 2 * (lax.rem(z + k, nz) * nq + mate)
                away = plane.astype(F32) - (depth - 1) / 2.0
                landing = column * cosr + away * sinr + centre
                w = jnp.maximum(0.0, 1.0 - jnp.abs(landing - height))
                weights[pl.ds(base, BOX), k * BOX:(k + 1) * BOX] = w.astype(BF16)
            return carry

        first = unit % 2 * (BINS // 2)
        lax.fori_loop(first, first + BINS // 2, one, 0)

    units = 2 * nq
    for step in range(steps):
        right(step).wait_recv()
        if step + PIECES < steps:
            right(step + PIECES).start()
        left(step).wait_recv()
        if step + PIECES < steps:
            left(step + PIECES).start()

    for k in range(1, nq):
        to_q(refs, s_pr, r_pr, k).wait_recv()
    for k in range(1, nz):
        to_z(meta_z, s_mz, r_mz, k).wait_recv()

    lanes = nz * PART

    def frame(r):
        return frames[:, r].reshape(lanes, BOX)

    def frame_pair(r):
        return jnp.concatenate([frame(2 * r), frame(2 * r + 1)], axis=1)

    def score(r, found):
        a = refs[:, r].reshape(nq * 2 * BINS, 2 * BOX)
        return found + dot_nt(a, jnp.concatenate([frame_pair(2 * r), frame_pair(2 * r + 1)], axis=0))

    found = jnp.zeros((nq * 2 * BINS, 2 * lanes), F32)
    found = lax.fori_loop(0, rows // 4, score, found, unroll=4).reshape(nq, 2, BINS, 2 * lanes)
    scores = found[:, 0, :, :lanes] + found[:, 1, :, lanes:]

    named = meta_z[0]
    for k in range(1, nz):
        named = named + meta_z[k]
    prior = meta_p[:, 0:8, :lanes]
    held, priors = [], []
    for t in range(2):
        place = named[t:t + 1, :lanes] - z * nq
        chosen = jnp.zeros((BINS, lanes), F32)
        chance = jnp.zeros((BINS, lanes), F32)
        for j in range(nq):
            chosen = jnp.where(place == j, scores[j], chosen)
            chance = jnp.where(place == j, prior[j], chance)
        partial[slab, t * BINS:(t + 1) * BINS, :] = chosen
        priors.append(chance)
        held.append((place >= 0) & (place < nq))

    def to_x(k):
        device = (me, lax.rem(slab + k, ns))
        return pltpu.make_async_remote_copy(
            partial.at[slab], partial.at[slab], s_x.at[k], r_x.at[k], device_id=device, device_id_type=MESH
        )

    for k in range(1, ns):
        to_x(k).start()
    for unit in range(units // 3):
        weigh(unit)
    for k in range(1, ns):
        to_x(k).wait_recv()
    scores = partial[0]
    for k in range(1, ns):
        scores = scores + partial[k]
    low = jnp.float32(-3.0e38)
    logits = [scores[t * BINS:(t + 1) * BINS] / BOX + priors[t] for t in range(2)]
    tops = [jnp.where(held[t], jnp.max(logits[t], axis=0, keepdims=True), low) for t in range(2)]
    top = jnp.maximum(tops[0], tops[1])
    summed = jnp.zeros((1, lanes), F32)
    for t in range(2):
        grown = jnp.exp(jnp.where(held[t], logits[t] - top, low))
        summed = summed + jnp.sum(grown, axis=0, keepdims=True)
    stats[z, 0:1, :lanes] = top
    stats[z, 1:2, :lanes] = summed
    for k in range(1, nz):
        to_z(stats, s_st, r_st, k).start()
    for unit in range(units // 3, units):
        weigh(unit)
    for step in range(steps):
        right(step).wait_send()
        left(step).wait_send()
    for k in range(1, nq):
        to_q(meta_p, s_mp, r_mp, k).wait_send()
        to_q(refs, s_pr, r_pr, k).wait_send()
    for k in range(1, ns):
        to_x(k).wait_send()
    for k in range(1, nz):
        to_z(meta_z, s_mz, r_mz, k).wait_send()
        to_z(stats, s_st, r_st, k).wait_recv()
    best = stats[0, 0:1, :lanes]
    for k in range(1, nz):
        best = jnp.maximum(best, stats[k, 0:1, :lanes])
    whole = jnp.zeros((1, lanes), F32)
    for k in range(nz):
        whole = whole + stats[k, 1:2, :lanes] * jnp.exp(stats[k, 0:1, :lanes] - best)
    norm = best + jnp.log(whole)
    chances = [jnp.exp(jnp.where(held[t], logits[t] - norm, low)) for t in range(2)]
    posterior = []
    for j in range(nq):
        value = jnp.zeros((BINS, lanes), F32)
        for t in range(2):
            place = named[t:t + 1, :lanes] - z * nq
            value = jnp.where(place == j, chances[t], value)
        posterior.append(value)
    posterior = jnp.concatenate(posterior, axis=0).astype(BF16)

    def average(r, carry):
        a = dot(posterior, frame_pair(r)).reshape(ny, 2, BINS, 2 * BOX)
        for which in range(2):
            share[which, :, 2 * r] = a[:, which, :, :BOX]
            share[which, :, 2 * r + 1] = a[:, which, :, BOX:]
        return carry

    half = rows // 2

    def to_core(k, h):
        place = at_y(k)[0]
        part = pl.ds(h * half, half)
        return pltpu.make_async_remote_copy(
            share.at[1 - core, place, part], from_core.at[place, part], s_rc.at[2 * k + h], r_rc.at[2 * k + h],
            device_id=other_core, device_id_type=MESH,
        )

    def to_owner(k, h):
        part = pl.ds(h * half // 2, half // 2)
        return pltpu.make_async_remote_copy(
            send_y.at[k, part], from_y.at[k, part], s_ry.at[2 * k + h], r_ry.at[2 * k + h],
            device_id=at_y(k)[1], device_id_type=MESH,
        )

    span = BINS * BOX
    mine = pl.multiple_of(q * span, span)

    def block_of(place, which):
        return pl.multiple_of((2 * place + which) * span, span)

    def along_y(k, h):
        ref = aver.at[pl.ds(2 * h * half, half), pl.ds(mine, span)]
        return pltpu.make_async_remote_copy(
            ref, ref, s_ay.at[2 * k + h], r_ay.at[2 * k + h], device_id=at_y(k)[1], device_id_type=MESH
        )

    def across(k, h):
        ref = aver.at[pl.ds(2 * h * half, 2 * half), pl.ds(block_of(lax.rem(y - k + ny, ny), core), span)]
        return pltpu.make_async_remote_copy(
            ref, ref, s_ac.at[2 * k + h], r_ac.at[2 * k + h], device_id=other_core, device_id_type=MESH
        )

    far_first = sorted(range(1, ny), key=lambda k: -min(k, ny - k))
    for h in range(2):
        lax.fori_loop(h * half // 2, (h + 1) * half // 2, average, 0, unroll=8)
        for k in far_first + [0]:
            to_core(k, h).start()
    for h in range(2):
        for k in far_first:
            place = at_y(k)[0]
            to_core(k, h).wait_recv()

            def pack(r, carry):
                a = share[core, place, 2 * r] + from_core[place, 2 * r]
                b = share[core, place, 2 * r + 1] + from_core[place, 2 * r + 1]
                send_y[k, r] = jnp.concatenate([a, b], axis=0).astype(BF16)
                return carry

            lax.fori_loop(h * half // 2, (h + 1) * half // 2, pack, 0, unroll=8)
            to_owner(k, h).start()

    mirror = (
        lax.broadcasted_iota(jnp.int32, (BOX, BOX), 0) + lax.broadcasted_iota(jnp.int32, (BOX, BOX), 1) == BOX - 1
    ).astype(F32).astype(BF16)

    def reverse(base, h):
        first = 2 * h * half
        tiles = [aver[first:first + half, pl.ds(pl.multiple_of(base + g * BOX, BOX), BOX)] for g in range(BINS)]
        turned = dot(jnp.concatenate(tiles, axis=0), mirror).astype(BF16)
        for g in range(BINS):
            at = pl.ds(pl.multiple_of(base + g * BOX, BOX), BOX)
            aver[first + half:first + 2 * half, at] = turned[g * half:(g + 1) * half]

    def add_up(r, carry):
        a = share[core, y, 2 * r] + from_core[y, 2 * r]
        b = share[core, y, 2 * r + 1] + from_core[y, 2 * r + 1]
        value = jnp.concatenate([a, b], axis=0)
        for k in range(1, ny):
            value = value + from_y[k, r].astype(F32)
        total[pl.ds(pl.multiple_of(r * 2 * BINS, 2 * BINS), 2 * BINS), :] = value
        return carry

    for h in range(2):
        to_core(0, h).wait_recv()
        for k in far_first[::-1]:
            to_owner(k, h).wait_recv()
        lax.fori_loop(h * half // 2, (h + 1) * half // 2, add_up, 0, unroll=8)
        for g in range(BINS):
            block = total[pl.ds(h * half * BINS + g, half, stride=BINS), :].astype(BF16)
            aver[2 * h * half:(2 * h + 1) * half, pl.ds(pl.multiple_of(mine + g * BOX, BOX), BOX)] = block
        for k in far_first:
            along_y(k, h).start()
        reverse(mine, h)
        across(0, h).start()

    def project(base, lanes_at):
        return dot(aver[:, pl.ds(base, span)], weights[pl.ds(base, span), lanes_at])

    def add_block(base, first):
        for pair in range(nz // 2):
            at = slice(2 * pair * BOX, (2 * pair + 2) * BOX)
            block = project(base, at)
            planes[:, at] = block if first else planes[:, at] + block

    def back(k, which):
        return block_of(lax.rem(y - k + ny, ny), which)

    near_first = far_first[::-1]
    add_block(back(0, core), True)
    for h in range(2):
        across(0, h).wait_recv()
    add_block(back(0, 1 - core), False)
    for k in near_first:
        along_y(k, 0).wait_recv()
        reverse(back(k, core), 0)
        across(k, 0).start()
    for k in near_first:
        along_y(k, 1).wait_recv()
        reverse(back(k, core), 1)
        across(k, 1).start()
        add_block(back(k, core), False)
    for k in near_first:
        for h in range(2):
            across(k, h).wait_recv()
        if k != near_first[-1]:
            add_block(back(k, 1 - core), False)
    final = back(near_first[-1], 1 - core)

    def even_copy(k):
        device = (lax.rem(z + k, nz) * nq + mate, slab)
        return pltpu.make_async_remote_copy(
            give_e.at[k], take_e.at[k], s_e.at[k], r_e.at[k], device_id=device, device_id_type=MESH
        )

    def odd_copy(k):
        device = ((nz - 1 - lax.rem(z + k, nz)) * nq + flip_q, slab)
        return pltpu.make_async_remote_copy(
            give_o.at[k], take_o.at[k], s_o.at[k], r_o.at[k], device_id=device, device_id_type=MESH
        )

    for turn in sorted(range(nz // 2), key=lambda turn: min(turn, nz // 2 - turn)):
        pair = lax.rem(nz // 4 - 1 + nz + turn - z, nz // 2)
        at = pl.ds(pl.multiple_of(2 * pair * BOX, 2 * BOX), 2 * BOX)
        block = (planes[:, at] + project(final, at)).reshape(2, 2, half, 2 * BOX)
        for k in range(2):
            give_o[2 * pair + k] = block[:, 1, :, k * BOX:(k + 1) * BOX].reshape(rows, BOX).astype(BF16)
            odd_copy(2 * pair + k).start()
        for k in range(2):
            give_e[2 * pair + k] = block[:, 0, :, k * BOX:(k + 1) * BOX].reshape(rows, BOX).astype(BF16)
            even_copy(2 * pair + k).start()

    for k in range(1, nz):
        to_z(stats, s_st, r_st, k).wait_send()
    for k in range(ny):
        for h in range(2):
            to_core(k, h).wait_send()
            across(k, h).wait_send()
            if k:
                to_owner(k, h).wait_send()
                along_y(k, h).wait_send()
    for k in range(nz):
        odd_copy(k).wait_send()
        even_copy(k).wait_send()
    value = jnp.zeros((rows, BOX), F32)
    for k in sorted(range(nz), key=lambda k: min(k, nz - k)):
        even_copy(k).wait_recv()
        value = value + take_e[k].astype(F32)
    out[0] = value
    for k in range(nz):
        odd_copy(k).wait_recv()
    out[1] = dot(
        jnp.concatenate([take_o[k] for k in range(nz)], axis=1), jnp.concatenate([mirror] * nz, axis=0)
    )


def body(nz, nq, ns, images, projections, regions, offsets, defocus, counts, tilt_angle):
    rows = BOX // ns
    pairs = rows // 2
    ny = nq // 2
    vmem = pl.BlockSpec(memory_space=pltpu.VMEM)
    dma = pltpu.SemaphoreType.DMA
    scratch = [
        pltpu.VMEM((PART, BOX, BOX), BF16),
        pltpu.VMEM((BINS, rows, BOX), BF16),
        pltpu.VMEM((3 * BOX, BOX), BF16),
        pltpu.VMEM((4 * PART * 8, BOX), F32),
        pltpu.VMEM((PART * rows, BOX), F32),
        pltpu.VMEM((nz, rows, PART, BOX), BF16),
        pltpu.VMEM((nq, rows // 4, 2 * BINS, 2 * BOX), BF16),
        pltpu.VMEM((nq, 24, BOX), F32),
        pltpu.VMEM((nz, 8, BOX), jnp.int32),
        pltpu.VMEM((ns, 2 * BINS, nz * PART), F32),
        pltpu.VMEM((nz, 8, BOX), F32),
        pltpu.VMEM((2, ny, rows, BINS, BOX), F32),
        pltpu.VMEM((ny, rows, BINS, BOX), F32),
        pltpu.VMEM((ny, pairs, 2 * BINS, BOX), BF16),
        pltpu.VMEM((ny, pairs, 2 * BINS, BOX), BF16),
        pltpu.VMEM((rows * BINS, BOX), F32),
        pltpu.VMEM((2 * rows, nq * BINS * BOX), BF16),
        pltpu.VMEM((nq * BINS * BOX, nz * BOX), BF16),
        pltpu.VMEM((2 * rows, nz * BOX), F32),
        pltpu.VMEM((nz, rows, BOX), BF16),
        pltpu.VMEM((nz, rows, BOX), BF16),
        pltpu.VMEM((nz, rows, BOX), BF16),
        pltpu.VMEM((nz, rows, BOX), BF16),
    ]
    scratch.append(dma((3,)))
    steps = PIECES * (nz - 1) // 2
    for count in (nq, nq, nz, steps, steps, ns, nz, 2 * ny, 2 * ny, 2 * ny, 2 * ny, nz, nz):
        scratch += [dma((count,)), dma((count,))]
    return pl.pallas_call(
        functools.partial(kernel, nz, nq, ns),
        out_shape=pltpu.VMEM((2, rows, BOX), F32),
        in_specs=[pl.BlockSpec(memory_space=pltpu.SMEM)] * 5 + [pl.BlockSpec(memory_space=pl.ANY)] * 3,
        out_specs=vmem,
        scratch_shapes=scratch,
        compiler_params=pltpu.CompilerParams(
            collective_id=0, has_side_effects=True, vmem_limit_bytes=60 * 1024 * 1024
        ),
    )(regions.T, offsets, defocus, counts, tilt_angle, images, projections, jnp.asarray(cosine_table()))


def solution(mesh):
    nq = PLANE_GROUP
    nz = mesh.shape["bins"] // nq
    ns = mesh.shape["slab"]
    in_specs = (
        P("bins", None, None),
        P("bins", None, None),
        P("bins", None),
        P(None, "bins"),
        P("bins"),
        P("bins"),
        P("bins"),
    )
    return jax.shard_map(
        functools.partial(body, nz, nq, ns),
        mesh=mesh,
        in_specs=in_specs,
        out_specs=P("bins", "slab", None),
        check_vma=False,
    )
```

```python
import functools

import jax
import jax.numpy as jnp
import ml_dtypes
import numpy as np
from jax import lax
from jax.experimental import pallas as pl
from jax.experimental.pallas import tpu as pltpu
from jax.sharding import PartitionSpec as P

AMP_COS = 0.1
AMP_SIN = 0.99498743710662
CHI_SCALE = 100.0
ENVELOPE = 8.0
BOX = 128
PART = 16
BINS = 8
PLANE_GROUP = 8
PIECES = 4
MESH = pl.DeviceIdType.MESH
F32 = jnp.float32
BF16 = jnp.bfloat16


def cosine_table():
    i = np.arange(BOX)
    cosine = np.cos(2.0 * np.pi / BOX * (i[:, None] * i[None, :] % BOX))
    high = cosine.astype(ml_dtypes.bfloat16)
    low = (cosine - high.astype(np.float64)).astype(ml_dtypes.bfloat16)
    return np.concatenate([high, high, low], axis=0)


def split(value):
    high = value.astype(BF16)
    return high, (value - high.astype(F32)).astype(BF16)


def dot(a, b):
    return jnp.dot(a, b, preferred_element_type=F32)


def dot_nt(a, b):
    return lax.dot_general(a, b, (((1,), (1,)), ((), ())), preferred_element_type=F32)


def kernel(
    nz, nq, ns,
    regions, offs, defocus, counts, tilt, images_hbm, proj_hbm, table_hbm,
    out,
    imgs, proj, table, taps, staged, frames, refs, meta_p, meta_z, partial, stats, share, from_core, send_y, from_y, total,
    aver, weights, planes, give_e, give_o, take_e, take_o,
    s_in, s_mp, r_mp, s_pr, r_pr, s_mz, r_mz, s_rt, r_rt, s_lf, r_lf, s_x, r_x, s_st, r_st,
    s_rc, r_rc, s_ry, r_ry, s_ac, r_ac, s_ay, r_ay, s_e, r_e, s_o, r_o,
):
    rows = BOX // ns
    pairs = rows // 2
    ny = nq // 2
    quarter = rows // PIECES
    depth = 2 * nz * nq
    me = lax.axis_index("bins")
    slab = lax.axis_index("slab")
    z = me // nq
    q = lax.rem(me, nq)
    y = q // 2
    core = lax.rem(q, 2)
    mate = q + 1 - 2 * core
    flip_q = nq - 1 - mate
    other_core = (z * nq + 2 * y + 1 - core, slab)
    centre = (BOX - 1) / 2.0

    def at_q(k):
        other = lax.rem(q + k, nq)
        return other, (z * nq + other, slab)

    def at_z(k):
        other = lax.rem(z + k, nz)
        return other, (other * nq + q, slab)

    def at_y(k):
        other = lax.rem(y + k, ny)
        return other, (z * nq + 2 * other + core, slab)

    first_row = pl.multiple_of(slab * rows, rows)
    loads = [
        pltpu.make_async_copy(src, dst, s_in.at[i])
        for i, (src, dst) in enumerate(
            (
                (table_hbm, table),
                (images_hbm, imgs),
                (proj_hbm.at[:, pl.ds(first_row, rows)], proj),
            )
        )
    ]
    for load in loads:
        load.start()

    barrier = pltpu.get_barrier_semaphore()
    partners = [at_q(k)[1] for k in range(1, nq)] + [at_z(k)[1] for k in range(1, nz)]
    partners += [(lax.rem(z + k, nz) * nq + other, slab) for k in range(1, nz) for other in (mate, flip_q)]
    partners += [(me, lax.rem(slab + k, ns)) for k in range(1, ns)]
    for device in partners:
        pl.semaphore_signal(barrier, inc=1, device_id=device, device_id_type=MESH)

    index = lax.broadcasted_iota(jnp.int32, (PART, BOX), 1)
    which = lax.broadcasted_iota(jnp.int32, (PART, BOX), 0)
    blur = jnp.zeros((PART, BOX), F32)
    for p in range(PART):
        blur = jnp.where(which == p, defocus[p], blur)
    freq = jnp.where(index < BOX // 2, index, index - BOX).astype(F32) / BOX
    square = freq * freq
    phase = CHI_SCALE * blur * square
    fade = jnp.exp(-ENVELOPE * square)
    sine, cosine = jnp.sin(phase), jnp.cos(phase)
    gains = jnp.concatenate(
        [
            -fade * (AMP_SIN * sine + AMP_COS * cosine),
            -fade * (AMP_SIN * cosine - AMP_COS * sine),
            fade * cosine,
            fade * sine,
        ],
        axis=0,
    )
    gh, gl = split(gains * (1.0 / BOX))
    loads[0].wait()
    found = dot(jnp.concatenate([gh, gl, gh], axis=1), table[...])
    for k in range(8):
        taps[pl.ds(k, 4 * PART, stride=8), :] = pltpu.roll(found, k, 1) if k else found

    def circulant(index, count, shift):
        eight = taps[pl.ds(pl.multiple_of(index * 8, 8), 8), :]
        return [pltpu.roll(eight, lax.rem(shift + 8 * k, BOX), 1) for k in range(count // 8)]

    def filter_one(p):
        down = lax.rem(slab * rows - offs[0, p] + 2 * BOX, BOX)
        along = lax.rem(offs[1, p] + BOX, BOX)
        left = jnp.concatenate(circulant(p, rows, down) + circulant(PART + p, rows, down), axis=0)
        t = dot(jnp.concatenate(split(left), axis=0), imgs[p])
        t = t[:2 * rows] + t[2 * rows:]
        t = jnp.concatenate([t[:rows], t[rows:]], axis=1)
        right = circulant(2 * PART + p, BOX, along) + circulant(3 * PART + p, BOX, along)
        right = jnp.concatenate(right, axis=0)
        out = dot(jnp.concatenate(split(t), axis=0), jnp.concatenate(split(right), axis=1))
        out = out[:, :BOX] + out[:, BOX:]
        staged[pl.ds(pl.multiple_of(p * rows, rows), rows), :] = out[:rows] + out[rows:]

    def filter_some(step, carry):
        for k in range(16):
            filter_one(step * 16 + k)
        return carry

    loads[1].wait()
    lax.fori_loop(0, PART // 16, filter_some, 0)
    for r in range(rows):
        frames[z, r] = staged[pl.ds(r, PART, stride=rows), :].astype(BF16)

    pl.semaphore_wait(barrier, len(partners))

    def to_q(buf, send, recv, k):
        device = at_q(k)[1]
        return pltpu.make_async_remote_copy(buf.at[q], buf.at[q], send.at[k], recv.at[k], device_id=device, device_id_type=MESH)

    def to_z(buf, send, recv, k):
        device = at_z(k)[1]
        ref = buf.at[z, pl.ds(0, 2)]
        return pltpu.make_async_remote_copy(ref, ref, send.at[k], recv.at[k], device_id=device, device_id_type=MESH)

    def ring(step, sign, send, recv):
        source = lax.rem(z + (nz - sign * (step // PIECES)), nz)
        piece = step % PIECES if sign > 0 else PIECES - 1 - step % PIECES
        ref = frames.at[source, pl.ds(piece * quarter, quarter)]
        device = (lax.rem(z + nz + sign, nz) * nq + q, slab)
        return pltpu.make_async_remote_copy(ref, ref, send.at[step], recv.at[step], device_id=device, device_id_type=MESH)

    def right(step):
        return ring(step, 1, s_rt, r_rt)

    def left(step):
        return ring(step, -1, s_lf, r_lf)

    steps = PIECES * (nz - 1) // 2
    for step in range(PIECES):
        right(step).start()
        left(step).start()

    lane = lax.broadcasted_iota(jnp.int32, (8, BOX), 1)
    line = lax.broadcasted_iota(jnp.int32, (8, BOX), 0)
    angle = jnp.zeros((8, BOX), F32)
    count = jnp.zeros((8, BOX), jnp.int32)
    for g in range(BINS):
        angle = jnp.where(line == g, tilt[g], angle)
        count = jnp.where(line == g, counts[g], count)
    meta_p[q, 0:8, :] = jnp.log(1.0 + count.astype(F32))
    meta_p[q, 8:16, :] = jnp.cos(angle)
    meta_p[q, 16:24, :] = jnp.sin(angle)
    named = jnp.zeros((8, BOX), jnp.int32)
    for p in range(PART):
        for t in range(2):
            named = jnp.where((lane == z * PART + p) & (line == t), regions[t, p], named)
    meta_z[z] = named

    for k in range(1, nq):
        to_q(meta_p, s_mp, r_mp, k).start()
    for k in range(1, nz):
        to_z(meta_z, s_mz, r_mz, k).start()
    loads[2].wait()
    for g in range(BINS):
        staged[g * rows:(g + 1) * rows, :] = proj[g].astype(F32)
    for r in range(rows // 4):
        lines = [staged[pl.ds(4 * r + k, BINS, stride=rows), :] for k in range(4)]
        upper, lower = jnp.concatenate(lines[:2], axis=1), jnp.concatenate(lines[2:], axis=1)
        refs[q, r] = jnp.concatenate([upper, lower], axis=0).astype(BF16)
    for k in range(1, nq):
        to_q(refs, s_pr, r_pr, k).start()
    for k in range(1, nq):
        to_q(meta_p, s_mp, r_mp, k).wait_recv()

    column = lax.broadcasted_iota(jnp.int32, (1, BOX), 1).astype(F32) - centre
    height = lax.broadcasted_iota(jnp.int32, (BOX, BOX), 0).astype(F32)

    def weigh(unit):
        j = unit // 2

        def one(g, carry):
            cosr = meta_p[j, pl.ds(8 + g, 1), :]
            sinr = meta_p[j, pl.ds(16 + g, 1), :]
            base = pl.multiple_of((j * BINS + g) * BOX, BOX)
            for k in range(nz):
                plane = 2 * (lax.rem(z + k, nz) * nq + mate)
                away = plane.astype(F32) - (depth - 1) / 2.0
                landing = column * cosr + away * sinr + centre
                w = jnp.maximum(0.0, 1.0 - jnp.abs(landing - height))
                weights[pl.ds(base, BOX), k * BOX:(k + 1) * BOX] = w.astype(BF16)
            return carry

        first = unit % 2 * (BINS // 2)
        lax.fori_loop(first, first + BINS // 2, one, 0)

    units = 2 * nq
    for step in range(steps):
        right(step).wait_recv()
        if step + PIECES < steps:
            right(step + PIECES).start()
        left(step).wait_recv()
        if step + PIECES < steps:
            left(step + PIECES).start()

    for k in range(1, nq):
        to_q(refs, s_pr, r_pr, k).wait_recv()
    for k in range(1, nz):
        to_z(meta_z, s_mz, r_mz, k).wait_recv()

    lanes = nz * PART

    def frame(r):
        return frames[:, r].reshape(lanes, BOX)

    def frame_pair(r):
        return jnp.concatenate([frame(2 * r), frame(2 * r + 1)], axis=1)

    def score(r, found):
        a = refs[:, r].reshape(nq * 2 * BINS, 2 * BOX)
        return found + dot_nt(a, jnp.concatenate([frame_pair(2 * r), frame_pair(2 * r + 1)], axis=0))

    found = jnp.zeros((nq * 2 * BINS, 2 * lanes), F32)
    found = lax.fori_loop(0, rows // 4, score, found, unroll=4).reshape(nq, 2, BINS, 2 * lanes)
    scores = found[:, 0, :, :lanes] + found[:, 1, :, lanes:]

    named = meta_z[0]
    for k in range(1, nz):
        named = named + meta_z[k]
    prior = meta_p[:, 0:8, :lanes]
    held, priors = [], []
    for t in range(2):
        place = named[t:t + 1, :lanes] - z * nq
        chosen = jnp.zeros((BINS, lanes), F32)
        chance = jnp.zeros((BINS, lanes), F32)
        for j in range(nq):
            chosen = jnp.where(place == j, scores[j], chosen)
            chance = jnp.where(place == j, prior[j], chance)
        partial[slab, t * BINS:(t + 1) * BINS, :] = chosen
        priors.append(chance)
        held.append((place >= 0) & (place < nq))

    def to_x(k):
        device = (me, lax.rem(slab + k, ns))
        return pltpu.make_async_remote_copy(
            partial.at[slab], partial.at[slab], s_x.at[k], r_x.at[k], device_id=device, device_id_type=MESH
        )

    for k in range(1, ns):
        to_x(k).start()
    for unit in range(units // 3):
        weigh(unit)
    for k in range(1, ns):
        to_x(k).wait_recv()
    scores = partial[0]
    for k in range(1, ns):
        scores = scores + partial[k]
    low = jnp.float32(-3.0e38)
    logits = [scores[t * BINS:(t + 1) * BINS] / BOX + priors[t] for t in range(2)]
    tops = [jnp.where(held[t], jnp.max(logits[t], axis=0, keepdims=True), low) for t in range(2)]
    top = jnp.maximum(tops[0], tops[1])
    summed = jnp.zeros((1, lanes), F32)
    for t in range(2):
        grown = jnp.exp(jnp.where(held[t], logits[t] - top, low))
        summed = summed + jnp.sum(grown, axis=0, keepdims=True)
    stats[z, 0:1, :lanes] = top
    stats[z, 1:2, :lanes] = summed
    for k in range(1, nz):
        to_z(stats, s_st, r_st, k).start()
    for unit in range(units // 3, units):
        weigh(unit)
    for step in range(steps):
        right(step).wait_send()
        left(step).wait_send()
    for k in range(1, nq):
        to_q(meta_p, s_mp, r_mp, k).wait_send()
        to_q(refs, s_pr, r_pr, k).wait_send()
    for k in range(1, ns):
        to_x(k).wait_send()
    for k in range(1, nz):
        to_z(meta_z, s_mz, r_mz, k).wait_send()
        to_z(stats, s_st, r_st, k).wait_recv()
    best = stats[0, 0:1, :lanes]
    for k in range(1, nz):
        best = jnp.maximum(best, stats[k, 0:1, :lanes])
    whole = jnp.zeros((1, lanes), F32)
    for k in range(nz):
        whole = whole + stats[k, 1:2, :lanes] * jnp.exp(stats[k, 0:1, :lanes] - best)
    norm = best + jnp.log(whole)
    chances = [jnp.exp(jnp.where(held[t], logits[t] - norm, low)) for t in range(2)]
    posterior = []
    for j in range(nq):
        value = jnp.zeros((BINS, lanes), F32)
        for t in range(2):
            place = named[t:t + 1, :lanes] - z * nq
            value = jnp.where(place == j, chances[t], value)
        posterior.append(value)
    posterior = jnp.concatenate(posterior, axis=0).astype(BF16)

    def average(r, carry):
        a = dot(posterior, frame_pair(r)).reshape(ny, 2, BINS, 2 * BOX)
        for which in range(2):
            share[which, :, 2 * r] = a[:, which, :, :BOX]
            share[which, :, 2 * r + 1] = a[:, which, :, BOX:]
        return carry

    half = rows // 2

    def to_core(k, h):
        place = at_y(k)[0]
        part = pl.ds(h * half, half)
        return pltpu.make_async_remote_copy(
            share.at[1 - core, place, part], from_core.at[place, part], s_rc.at[2 * k + h], r_rc.at[2 * k + h],
            device_id=other_core, device_id_type=MESH,
        )

    def to_owner(k, h):
        part = pl.ds(h * half // 2, half // 2)
        return pltpu.make_async_remote_copy(
            send_y.at[k, part], from_y.at[k, part], s_ry.at[2 * k + h], r_ry.at[2 * k + h],
            device_id=at_y(k)[1], device_id_type=MESH,
        )

    span = BINS * BOX
    mine = pl.multiple_of(q * span, span)

    def block_of(place, which):
        return pl.multiple_of((2 * place + which) * span, span)

    def along_y(k, h):
        ref = aver.at[pl.ds(2 * h * half, half), pl.ds(mine, span)]
        return pltpu.make_async_remote_copy(
            ref, ref, s_ay.at[2 * k + h], r_ay.at[2 * k + h], device_id=at_y(k)[1], device_id_type=MESH
        )

    def across(k, h):
        ref = aver.at[pl.ds(2 * h * half, 2 * half), pl.ds(block_of(lax.rem(y - k + ny, ny), core), span)]
        return pltpu.make_async_remote_copy(
            ref, ref, s_ac.at[2 * k + h], r_ac.at[2 * k + h], device_id=other_core, device_id_type=MESH
        )

    far_first = sorted(range(1, ny), key=lambda k: -min(k, ny - k))
    for h in range(2):
        lax.fori_loop(h * half // 2, (h + 1) * half // 2, average, 0, unroll=8)
        for k in far_first + [0]:
            to_core(k, h).start()
    for h in range(2):
        for k in far_first:
            place = at_y(k)[0]
            to_core(k, h).wait_recv()

            def pack(r, carry):
                a = share[core, place, 2 * r] + from_core[place, 2 * r]
                b = share[core, place, 2 * r + 1] + from_core[place, 2 * r + 1]
                send_y[k, r] = jnp.concatenate([a, b], axis=0).astype(BF16)
                return carry

            lax.fori_loop(h * half // 2, (h + 1) * half // 2, pack, 0, unroll=8)
            to_owner(k, h).start()

    mirror = (
        lax.broadcasted_iota(jnp.int32, (BOX, BOX), 0) + lax.broadcasted_iota(jnp.int32, (BOX, BOX), 1) == BOX - 1
    ).astype(F32).astype(BF16)

    def reverse(base, h):
        first = 2 * h * half
        tiles = [aver[first:first + half, pl.ds(pl.multiple_of(base + g * BOX, BOX), BOX)] for g in range(BINS)]
        turned = dot(jnp.concatenate(tiles, axis=0), mirror).astype(BF16)
        for g in range(BINS):
            at = pl.ds(pl.multiple_of(base + g * BOX, BOX), BOX)
            aver[first + half:first + 2 * half, at] = turned[g * half:(g + 1) * half]

    def add_up(r, carry):
        a = share[core, y, 2 * r] + from_core[y, 2 * r]
        b = share[core, y, 2 * r + 1] + from_core[y, 2 * r + 1]
        value = jnp.concatenate([a, b], axis=0)
        for k in range(1, ny):
            value = value + from_y[k, r].astype(F32)
        total[pl.ds(pl.multiple_of(r * 2 * BINS, 2 * BINS), 2 * BINS), :] = value
        return carry

    for h in range(2):
        to_core(0, h).wait_recv()
        for k in far_first[::-1]:
            to_owner(k, h).wait_recv()
        lax.fori_loop(h * half // 2, (h + 1) * half // 2, add_up, 0, unroll=8)
        for g in range(BINS):
            block = total[pl.ds(h * half * BINS + g, half, stride=BINS), :].astype(BF16)
            aver[2 * h * half:(2 * h + 1) * half, pl.ds(pl.multiple_of(mine + g * BOX, BOX), BOX)] = block
        for k in far_first:
            along_y(k, h).start()
        reverse(mine, h)
        across(0, h).start()

    def project(base, lanes_at):
        return dot(aver[:, pl.ds(base, span)], weights[pl.ds(base, span), lanes_at])

    def add_block(base, first):
        for pair in range(nz // 2):
            at = slice(2 * pair * BOX, (2 * pair + 2) * BOX)
            block = project(base, at)
            planes[:, at] = block if first else planes[:, at] + block

    def back(k, which):
        return block_of(lax.rem(y - k + ny, ny), which)

    near_first = far_first[::-1]
    add_block(back(0, core), True)
    for h in range(2):
        across(0, h).wait_recv()
    add_block(back(0, 1 - core), False)
    for k in near_first:
        along_y(k, 0).wait_recv()
        reverse(back(k, core), 0)
        across(k, 0).start()
    for k in near_first:
        along_y(k, 1).wait_recv()
        reverse(back(k, core), 1)
        across(k, 1).start()
        add_block(back(k, core), False)
    for k in near_first:
        for h in range(2):
            across(k, h).wait_recv()
        if k != near_first[-1]:
            add_block(back(k, 1 - core), False)
    final = back(near_first[-1], 1 - core)

    def even_copy(k):
        device = (lax.rem(z + k, nz) * nq + mate, slab)
        return pltpu.make_async_remote_copy(
            give_e.at[k], take_e.at[k], s_e.at[k], r_e.at[k], device_id=device, device_id_type=MESH
        )

    def odd_copy(k):
        device = ((nz - 1 - lax.rem(z + k, nz)) * nq + flip_q, slab)
        return pltpu.make_async_remote_copy(
            give_o.at[k], take_o.at[k], s_o.at[k], r_o.at[k], device_id=device, device_id_type=MESH
        )

    for turn in sorted(range(nz // 2), key=lambda turn: min(turn, nz // 2 - turn)):
        pair = lax.rem(nz // 4 - 1 + nz + turn - z, nz // 2)
        at = pl.ds(pl.multiple_of(2 * pair * BOX, 2 * BOX), 2 * BOX)
        block = (planes[:, at] + project(final, at)).reshape(2, 2, half, 2 * BOX)
        for k in range(2):
            give_o[2 * pair + k] = block[:, 1, :, k * BOX:(k + 1) * BOX].reshape(rows, BOX).astype(BF16)
            odd_copy(2 * pair + k).start()
        for k in range(2):
            give_e[2 * pair + k] = block[:, 0, :, k * BOX:(k + 1) * BOX].reshape(rows, BOX).astype(BF16)
            even_copy(2 * pair + k).start()

    for k in range(1, nz):
        to_z(stats, s_st, r_st, k).wait_send()
    for k in range(ny):
        for h in range(2):
            to_core(k, h).wait_send()
            across(k, h).wait_send()
            if k:
                to_owner(k, h).wait_send()
                along_y(k, h).wait_send()
    for k in range(nz):
        odd_copy(k).wait_send()
        even_copy(k).wait_send()
    value = jnp.zeros((rows, BOX), F32)
    for k in sorted(range(nz), key=lambda k: min(k, nz - k)):
        even_copy(k).wait_recv()
        value = value + take_e[k].astype(F32)
    out[0] = value
    for k in range(nz):
        odd_copy(k).wait_recv()
    out[1] = dot(
        jnp.concatenate([take_o[k] for k in range(nz)], axis=1), jnp.concatenate([mirror] * nz, axis=0)
    )


def body(nz, nq, ns, images, projections, regions, offsets, defocus, counts, tilt_angle):
    rows = BOX // ns
    pairs = rows // 2
    ny = nq // 2
    vmem = pl.BlockSpec(memory_space=pltpu.VMEM)
    dma = pltpu.SemaphoreType.DMA
    scratch = [
        pltpu.VMEM((PART, BOX, BOX), BF16),
        pltpu.VMEM((BINS, rows, BOX), BF16),
        pltpu.VMEM((3 * BOX, BOX), BF16),
        pltpu.VMEM((4 * PART * 8, BOX), F32),
        pltpu.VMEM((PART * rows, BOX), F32),
        pltpu.VMEM((nz, rows, PART, BOX), BF16),
        pltpu.VMEM((nq, rows // 4, 2 * BINS, 2 * BOX), BF16),
        pltpu.VMEM((nq, 24, BOX), F32),
        pltpu.VMEM((nz, 8, BOX), jnp.int32),
        pltpu.VMEM((ns, 2 * BINS, nz * PART), F32),
        pltpu.VMEM((nz, 8, BOX), F32),
        pltpu.VMEM((2, ny, rows, BINS, BOX), F32),
        pltpu.VMEM((ny, rows, BINS, BOX), F32),
        pltpu.VMEM((ny, pairs, 2 * BINS, BOX), BF16),
        pltpu.VMEM((ny, pairs, 2 * BINS, BOX), BF16),
        pltpu.VMEM((rows * BINS, BOX), F32),
        pltpu.VMEM((2 * rows, nq * BINS * BOX), BF16),
        pltpu.VMEM((nq * BINS * BOX, nz * BOX), BF16),
        pltpu.VMEM((2 * rows, nz * BOX), F32),
        pltpu.VMEM((nz, rows, BOX), BF16),
        pltpu.VMEM((nz, rows, BOX), BF16),
        pltpu.VMEM((nz, rows, BOX), BF16),
        pltpu.VMEM((nz, rows, BOX), BF16),
    ]
    scratch.append(dma((3,)))
    steps = PIECES * (nz - 1) // 2
    for count in (nq, nq, nz, steps, steps, ns, nz, 2 * ny, 2 * ny, 2 * ny, 2 * ny, nz, nz):
        scratch += [dma((count,)), dma((count,))]
    return pl.pallas_call(
        functools.partial(kernel, nz, nq, ns),
        out_shape=pltpu.VMEM((2, rows, BOX), F32),
        in_specs=[pl.BlockSpec(memory_space=pltpu.SMEM)] * 5 + [pl.BlockSpec(memory_space=pl.ANY)] * 3,
        out_specs=vmem,
        scratch_shapes=scratch,
        compiler_params=pltpu.CompilerParams(
            collective_id=0, has_side_effects=True, vmem_limit_bytes=60 * 1024 * 1024
        ),
    )(regions.T, offsets, defocus, counts, tilt_angle, images, projections, jnp.asarray(cosine_table()))


def solution(mesh):
    nq = PLANE_GROUP
    nz = mesh.shape["bins"] // nq
    ns = mesh.shape["slab"]
    in_specs = (
        P("bins", None, None),
        P("bins", None, None),
        P("bins", None),
        P(None, "bins"),
        P("bins"),
        P("bins"),
        P("bins"),
    )
    return jax.shard_map(
        functools.partial(body, nz, nq, ns),
        mesh=mesh,
        in_specs=in_specs,
        out_specs=P("bins", "slab", None),
        check_vma=False,
    )
```
